32 devices in a mesh: row: 2 (over x), col: 16 (over z, y, core).
Axes of the slice: x: 2, y: 2, z: 4, core: 2. Of those that a mesh axis runs over, the one named last changes fastest.
Arguments:
- object_field: float32 [2, 512, 4096], P(None, 'row', 'col'), may hold values from -6 to 6
- probe: float32 [2, 4, 128, 128], replicated, may hold values from -6 to 6
- patterns: bfloat16 [2, 16, 8, 128, 128], P('row', 'col'), may hold values from 0.5 to 2
- row_scales: float32 [2, 16, 8, 128], P('row', 'col'), may hold values from 0.3 to 3
- positions: int32 [2, 16, 8, 2], P('row', 'col'), may hold values from 0 to 255
- counts: int32 [2, 16], P('row', 'col'), may hold values from 4 to 8, as said below
Outputs:
- object_out: float32 [2, 512, 4096], P(None, 'row', 'col')
- probe_out: float32 [2, 4, 128, 128], replicated
The draws below stay inside these ranges and needn't reach their ends.
Inputs may be any that keep to these rules, and one draw needn't show every extreme that they name: positions p >= counts[a,b] of tile (a,b) are ignored; some tile has all 8 positions live.
All inputs are finite; a program needn't handle non-finite values.
Results may differ from the reference program's by a relative error of at most 0.0003.
Values sent between devices are 32-bit elements; how exact they have to be, the bound alone decides.
A program may use at most 128 MiB of HBM per device.

```python
import math
import jax
import jax.numpy as jnp
from jax import lax

PIX = 128
MODES = 4
POS = 8
PASSES = 2
TILE = 256
OBJ_ROWS = 512
OBJ_COLS = 4096
N_ROW = 2
N_COL = 16


def draw_counts(key, part):
    key_counts, key_full = jax.random.split(key)
    drawn = jax.random.randint(key_counts, (N_ROW * N_COL,), POS // 2, POS + 1)
    chosen = jax.random.randint(key_full, (), 0, N_ROW * N_COL)
    flattened = jnp.where(jnp.arange(N_ROW * N_COL) == chosen, POS, drawn)
    return flattened.reshape(N_ROW, N_COL).astype(jnp.int32)


def touch_ends(values, rng, low, high):
    place = [jax.random.randint(jax.random.fold_in(rng, axis), (), 0, length) for axis, length in enumerate(values.shape)]
    widest = values.shape.index(max(values.shape))
    beside = place[:widest] + [(place[widest] + 1) % values.shape[widest]] + place[widest + 1:]
    return values.at[tuple(place)].set(low).at[tuple(beside)].set(high)


def block_scale(rng, shape, pieces, low, high):
    def one(axis_at, shards_of):
        heights = jax.random.uniform(jax.random.fold_in(jax.random.fold_in(rng, 6), axis_at), (shards_of,), jnp.float32, low / len(pieces), high / len(pieces))
        return jnp.repeat(jnp.exp(heights), shape[axis_at] // shards_of).reshape((-1,) + (1,) * (len(shape) - axis_at - 1))

    level = one(*pieces[0])
    for cut in pieces[1:]:
        level = level * one(*cut)
    return level


def bell_draw(key, dims, deviation, limit, shards=(), kind=jnp.bfloat16):
    loudness = block_scale(key, dims, shards, -0.22, 0.18) if shards else 1.0
    entries = jax.random.normal(key, dims, jnp.float32) * deviation * loudness
    return jnp.minimum(jnp.maximum(entries, -limit), limit).astype(kind)


def setup_inputs(seed: int = 0) -> dict:
    streams_of = jax.random.split(jax.random.key(seed), 7)
    return {
        "object_field": bell_draw(streams_of[0], (2, OBJ_ROWS, OBJ_COLS), 1.0, 6.0, ((1, 2), (2, 16)), jnp.float32),
        "probe": bell_draw(streams_of[1], (2, MODES, PIX, PIX), 1.0, 6.0, (), jnp.float32),
        "patterns": jnp.clip(0.5 + 1.5 * jax.random.uniform(streams_of[2], (N_ROW, N_COL, POS, PIX, PIX), jnp.float32) ** block_scale(streams_of[2], (N_ROW, N_COL, POS, PIX, PIX), ((0, 2), (1, 16)), -0.2, 0.2), 0.5, 2.0).astype(jnp.bfloat16),
        "row_scales": jnp.clip(jnp.exp(math.log(3.0) - 2.3025851 * jax.random.uniform(streams_of[3], (N_ROW, N_COL, POS, PIX), jnp.float32) ** block_scale(streams_of[3], (N_ROW, N_COL, POS, PIX), ((0, 2), (1, 16)), -0.2, 0.2)), 0.3, 3.0),
        "positions": touch_ends(jax.random.randint(streams_of[4], (N_ROW, N_COL, POS, 2), 0, TILE), jax.random.fold_in(streams_of[4], 1), 0, TILE - 1).astype(jnp.int32),
        "counts": draw_counts(jax.random.fold_in(streams_of[6], 71), 0),
    }


def reference(object_field, probe, patterns, row_scales, positions, counts):
    half_width = PIX // 2
    object_now = object_field[0] + 1j * object_field[1]
    probe_now = probe[0] + 1j * probe[1]
    amplitudes = (patterns.astype(jnp.float32) * row_scales[..., None]).reshape(-1, PIX, PIX)
    tile_rows = jnp.broadcast_to((jnp.arange(N_ROW, dtype=jnp.int32) * TILE)[:, None, None], (N_ROW, N_COL, POS))
    tile_cols = jnp.broadcast_to((jnp.arange(N_COL, dtype=jnp.int32) * TILE)[None, :, None], (N_ROW, N_COL, POS))
    row_starts = (tile_rows + positions[..., 0]).reshape(-1).astype(jnp.int32)
    col_starts = (tile_cols + positions[..., 1]).reshape(-1).astype(jnp.int32)
    live_flag = (jnp.arange(POS, dtype=jnp.int32)[None, None, :] < counts[:, :, None]).astype(object_field.dtype).reshape(-1)
    for pass_number in range(PASSES):
        padded = jnp.pad(object_now, half_width)

        def one_position(running, element):
            updates, gradient, weight = running
            row_at, col_at, live_now, amplitude = element
            object_patch = lax.dynamic_slice(padded, (row_at, col_at), (PIX, PIX))
            exit_wave = probe_now * object_patch[None]
            far_field = jnp.fft.fft2(exit_wave, norm='ortho')
            intensity = lax.optimization_barrier(jnp.sum(jnp.real(far_field) ** 2 + jnp.imag(far_field) ** 2, axis=0))
            factor = amplitude / jnp.maximum(jnp.sqrt(intensity), 0.5)
            back_wave = jnp.fft.ifft2(far_field * factor[None], norm='ortho')
            difference = (back_wave - exit_wave) * live_now
            contribution = lax.optimization_barrier(jnp.sum(jnp.conj(probe_now) * difference, axis=0))
            current = lax.dynamic_slice(updates, (row_at, col_at), (PIX, PIX))
            updates = lax.dynamic_update_slice(updates, current + contribution, (row_at, col_at))
            gradient = gradient + jnp.conj(object_patch)[None] * difference
            weight = weight + live_now * (jnp.real(object_patch) ** 2 + jnp.imag(object_patch) ** 2)
            return ((updates, gradient, weight), None)
        initial = (jnp.zeros_like(padded), jnp.zeros_like(probe_now), jnp.zeros((PIX, PIX), object_field.dtype))
        (updates, gradient, weight), unused = lax.scan(one_position, initial, (row_starts, col_starts, live_flag, amplitudes))
        probe_peak = jnp.max(lax.optimization_barrier(jnp.sum(jnp.real(probe_now) ** 2 + jnp.imag(probe_now) ** 2, axis=0)))
        object_now = object_now + updates[half_width:-half_width, half_width:-half_width] / probe_peak
        probe_now = probe_now + gradient / weight[None]
    object_out = jnp.stack([jnp.real(object_now), jnp.imag(object_now)])
    probe_out = jnp.stack([jnp.real(probe_now), jnp.imag(probe_now)])
    return (object_out, probe_out)
```

```python
import functools
import math

import jax
import jax.numpy as jnp
import numpy as np
from jax import lax
from jax.experimental import pallas as pl
from jax.experimental.pallas import tpu as pltpu
from jax.sharding import PartitionSpec as P

PASSES = 2
MESH = pl.DeviceIdType.MESH
VMEM = pl.BlockSpec(memory_space=pltpu.VMEM)
SMEM = pl.BlockSpec(memory_space=pltpu.SMEM)
LIMIT = 48 * 1024 * 1024


def dft_tables(length):
    index = np.arange(length)
    angle = (index[:, None] * index[None, :] % length) * (2.0 * math.pi / length)
    cosine, sine = np.cos(angle), np.sin(angle)
    forward = np.block([[cosine, -sine], [sine, cosine]]).astype(np.float32)
    inverse = np.block([[cosine, sine], [-sine, cosine]]).astype(np.float32)
    out = []
    for table in (forward, inverse):
        high = table.astype(jnp.bfloat16)
        out += [high, (table - high.astype(np.float32)).astype(jnp.bfloat16)]
    return out


def split(value):
    high = value.astype(jnp.bfloat16)
    return high, (value - high.astype(jnp.float32)).astype(jnp.bfloat16)


def dot(a, b):
    return jnp.dot(a, b, preferred_element_type=jnp.float32)


def times_table(value, high, low):
    top, rest = split(value)
    return dot(top, high[...]) + dot(rest, high[...]) + dot(top, low[...])


def table_times(high, low, value):
    top, rest = split(value)
    return dot(high[...], top) + dot(high[...], rest) + dot(low[...], top)


def pass_kernel(
    pos, count, ext, probe, amp, fwd_hi, fwd_lo, inv_hi, inv_lo, upd, sums, power, far, wave
):
    modes, pix = probe.shape[1], probe.shape[2]
    group = 2 if modes % 2 == 0 else 1
    upd[...] = jnp.zeros_like(upd)
    sums[...] = jnp.zeros_like(sums)
    power[...] = jnp.sum(probe[0] * probe[0] + probe[1] * probe[1], axis=0)

    def body(p, carry):
        row, col = pos[p, 0], pos[p, 1]
        lane = pl.multiple_of(col // pix * pix, pix)
        shift = lax.rem(col, pix)
        down = lax.rem(row, 8)
        tall = pix + 8
        rows, lanes = pl.ds(pl.multiple_of(row // 8 * 8, 8), tall), pl.ds(lane, 2 * pix)
        back_by = lax.rem(2 * pix - shift, 2 * pix)
        up_by = lax.rem(tall - down, tall)

        def window(plane):
            aligned = pltpu.roll(ext[plane, rows, lanes], back_by, 1)[:, :pix]
            return pltpu.roll(aligned, up_by, 0)[:pix]

        o_re, o_im = window(0), window(1)
        wave[0] = o_re
        wave[1] = o_im
        intensity = jnp.zeros((pix, pix), jnp.float32)
        for first in range(0, modes, group):
            exits = []
            for m in range(first, first + group):
                p_re, p_im = probe[0, m], probe[1, m]
                exits.append(
                    jnp.concatenate([p_re * o_re - p_im * o_im, p_re * o_im + p_im * o_re], 1)
                )
            half = times_table(jnp.concatenate(exits, 0), fwd_hi, fwd_lo)
            parts = [half[k * pix : (k + 1) * pix] for k in range(group)]
            stacked = jnp.concatenate(
                [jnp.concatenate([x[:, :pix], x[:, pix:]], 0) for x in parts], 1
            )
            full = table_times(inv_hi, inv_lo, stacked)
            far[:, first * pix : (first + group) * pix] = full
            for k in range(group):
                block = full[:, k * pix : (k + 1) * pix]
                intensity += block[:pix] * block[:pix] + block[pix:] * block[pix:]
        size = jnp.maximum(jnp.sqrt(intensity) * (1.0 / pix), 0.5)
        factor = amp[p] / size * (1.0 / (pix * pix))
        both = jnp.concatenate([factor, factor], 0)
        o_re, o_im = wave[0], wave[1]
        c_re = -power[...] * o_re
        c_im = -power[...] * o_im
        for first in range(0, modes, group):
            spread = jnp.concatenate([both] * group, 1)
            scaled = far[:, first * pix : (first + group) * pix] * spread
            half = table_times(fwd_hi, fwd_lo, scaled)
            parts = [half[:, k * pix : (k + 1) * pix] for k in range(group)]
            flat = jnp.concatenate(
                [jnp.concatenate([x[:pix], x[pix:]], 1) for x in parts], 0
            )
            back = times_table(flat, inv_hi, inv_lo)
            for k in range(group):
                m = first + k
                b_re = back[k * pix : (k + 1) * pix, :pix]
                b_im = back[k * pix : (k + 1) * pix, pix:]
                p_re, p_im = probe[0, m], probe[1, m]
                c_re += p_re * b_re + p_im * b_im
                c_im += p_re * b_im - p_im * b_re
                sums[m] += o_re * b_re + o_im * b_im
                sums[modes + m] += o_re * b_im - o_im * b_re
        sums[2 * modes] += o_re * o_re + o_im * o_im
        for plane, value in enumerate((c_re, c_im)):
            moved = pltpu.roll(jnp.concatenate([value, jnp.zeros((8, pix), jnp.float32)], 0), down, 0)
            moved = jnp.concatenate([moved, jnp.zeros_like(moved)], 1)
            upd[plane, rows, lanes] += pltpu.roll(moved, shift, 1)
        return carry

    lax.fori_loop(0, count[0, 0], body, 0)


def run_pass(ext, probe, amp, starts, counts, tables, rows_padded):
    modes, pix = probe.shape[1], probe.shape[2]
    planes = rows_padded // pix
    return pl.pallas_call(
        pass_kernel,
        out_shape=(
            jax.ShapeDtypeStruct(ext.shape, jnp.float32),
            jax.ShapeDtypeStruct((planes, pix, pix), jnp.float32),
        ),
        in_specs=[SMEM, SMEM] + [VMEM] * 7,
        out_specs=(VMEM, VMEM),
        scratch_shapes=[
            pltpu.VMEM((pix, pix), jnp.float32),
            pltpu.VMEM((2 * pix, modes * pix), jnp.float32),
            pltpu.VMEM((2, pix, pix), jnp.float32),
        ],
        compiler_params=pltpu.CompilerParams(vmem_limit_bytes=LIMIT),
        name="scan_pass",
    )(starts, counts, ext, probe, amp, *tables)


def col_factors(count):
    core = math.gcd(2, count)
    far = math.gcd(4, count // core)
    return [f for f in (core, count // core // far, far) if f > 1]


class Edges:
    def __init__(self, axis, send_sem, recv_sem):
        self.axis = axis
        self.count = lax.axis_size(axis)
        self.me = lax.axis_index(axis)
        self.has_low = self.me > 0
        self.has_high = self.me < self.count - 1
        self.sems = (send_sem, recv_sem)

    def greet(self, barrier):
        @pl.when(self.has_low)
        def _():
            pl.semaphore_signal(
                barrier, inc=1, device_id={self.axis: self.me - 1}, device_id_type=MESH
            )

        @pl.when(self.has_high)
        def _():
            pl.semaphore_signal(
                barrier, inc=1, device_id={self.axis: self.me + 1}, device_id_type=MESH
            )

        return self.has_low.astype(jnp.int32) + self.has_high.astype(jnp.int32)

    def copies(self, low_src, high_src, from_low, from_high):
        send, recv = self.sems

        def make(src, dst, slot, target):
            return pltpu.make_async_remote_copy(
                src_ref=src,
                dst_ref=dst,
                send_sem=send.at[slot],
                recv_sem=recv.at[slot],
                device_id={self.axis: target},
                device_id_type=MESH,
            )

        self.up = make(high_src, from_low, 0, self.me + 1)
        self.down = make(low_src, from_high, 1, self.me - 1)

    def start(self):
        @pl.when(self.has_high)
        def _():
            self.up.start()

        @pl.when(self.has_low)
        def _():
            self.down.start()

    def finish(self, add_low, add_high):
        @pl.when(self.has_low)
        def _():
            self.up.wait_recv()
            add_low()

        @pl.when(self.has_high)
        def _():
            self.down.wait_recv()
            add_high()

    def drain(self):
        @pl.when(self.has_high)
        def _():
            self.up.wait_send()

        @pl.when(self.has_low)
        def _():
            self.down.wait_send()


def exchange_kernel(
    kind, rim, modes, pix, *refs
):
    reduce = kind != "rim"
    if reduce:
        (upd, ext, probe, sums, ext_out, probe_out) = refs[:6]
        scratch = refs[6:]
    else:
        upd, ext_out = refs[:2]
        scratch = refs[2:]
    work, low_r, high_r, low_c, high_c, send_e, recv_e = scratch[:7]
    full_rows, full_cols = work.shape[1], work.shape[2]
    row_edges = Edges("row", send_e.at[0], recv_e.at[0])
    col_edges = Edges("col", send_e.at[1], recv_e.at[1])
    wide = 2 * rim
    if kind == "rim":
        send_high, send_low = (full_rows - wide, rim), (rim, rim)
        put_low, put_high = (0, rim), (full_rows - rim, rim)
    elif kind == "all":
        send_high, send_low = (full_rows - wide, wide), (0, wide)
        put_low, put_high = (0, wide), (full_rows - wide, wide)
    else:
        send_high, send_low = (full_rows - rim, rim), (0, rim)
        put_low, put_high = (rim, rim), (full_rows - wide, rim)
    row_span = (rim, full_rows - wide) if kind == "tile" else (0, full_rows)

    barrier = pltpu.get_barrier_semaphore()
    greeted = row_edges.greet(barrier) + col_edges.greet(barrier)
    n_row, n_col = lax.axis_size("row"), lax.axis_size("col")
    me_row, me_col = lax.axis_index("row"), lax.axis_index("col")
    stages = []
    if reduce:
        stride = 1
        for size in col_factors(n_col):
            mine = lax.rem(me_col // stride, size)
            base = me_col - mine * stride
            others = [lax.rem(mine + d, size) for d in range(1, size)]
            stages.append((size, mine, [(q, base + q * stride) for q in others]))
            stride *= size
        row_others = [lax.rem(me_row + d, n_row) for d in range(1, n_row)]
        for _, _, others in stages:
            for _, target in others:
                pl.semaphore_signal(barrier, inc=1, device_id={"col": target}, device_id_type=MESH)
        for target in row_others:
            pl.semaphore_signal(barrier, inc=1, device_id={"row": target}, device_id_type=MESH)
        greeted = greeted + sum(len(s[2]) for s in stages) + len(row_others)
    pl.semaphore_wait(barrier, greeted)

    row_edges.copies(
        upd.at[:, pl.ds(*send_low), :], upd.at[:, pl.ds(*send_high), :], low_r, high_r
    )
    row_edges.start()

    def finish_rows():
        work[...] = upd[...]

        def add_low():
            work[:, pl.ds(*put_low), :] += low_r[...]

        def add_high():
            work[:, pl.ds(*put_high), :] += high_r[...]

        row_edges.finish(add_low, add_high)
        col_edges.copies(
            work.at[:, pl.ds(*row_span), pl.ds(0, wide)],
            work.at[:, pl.ds(*row_span), pl.ds(full_cols - wide, wide)],
            low_c,
            high_c,
        )
        col_edges.start()

    def finish_cols():
        ext_out[...] = work[...]

        def add_low():
            ext_out[:, pl.ds(*row_span), pl.ds(0, wide)] += low_c[...]

        def add_high():
            ext_out[:, pl.ds(*row_span), pl.ds(full_cols - wide, wide)] += high_c[...]

        col_edges.finish(add_low, add_high)

    if not reduce:
        finish_rows()
        finish_cols()
        row_edges.drain()
        col_edges.drain()
        return

    acc, gat, row_in, send_s, recv_s, send_g, recv_g, send_x, recv_x = scratch[7:16]
    landings = scratch[16:]
    pending = []
    offset, length, slot = 0, acc.shape[0], 0
    acc[...] = sums[...].reshape(acc.shape)
    spans = []
    for index, (size, mine, others) in enumerate(stages):
        piece = length // size
        spans.append((offset, piece, slot))
        copies = []
        for d, (q, target) in enumerate(others):
            copy = pltpu.make_async_remote_copy(
                src_ref=acc.at[pl.ds(pl.multiple_of(offset + q * piece, 8), piece)],
                dst_ref=landings[index].at[d],
                send_sem=send_s.at[slot],
                recv_sem=recv_s.at[slot],
                device_id={"col": target},
                device_id_type=MESH,
            )
            slot += 1
            copy.start()
            copies.append(copy)
        if index == 1 or len(stages) == 1:
            finish_rows()
        keep = pl.ds(pl.multiple_of(offset + mine * piece, 8), piece)
        total = acc[keep, :]
        for d, copy in enumerate(copies):
            copy.wait_recv()
            total = total + landings[index][d]
        acc[keep, :] = total
        pending += copies
        offset, length = offset + mine * piece, piece

    keep = pl.ds(pl.multiple_of(offset, 8), length)
    copies = []
    for d, target in enumerate(row_others):
        copy = pltpu.make_async_remote_copy(
            src_ref=acc.at[keep],
            dst_ref=row_in.at[d],
            send_sem=send_x.at[d],
            recv_sem=recv_x.at[d],
            device_id={"row": target},
            device_id_type=MESH,
        )
        copy.start()
        copies.append(copy)
    for copy in copies:
        copy.wait_recv()
    total = None
    for r in range(n_row):
        term = None
        for d in range(n_row - 1):
            is_it = lax.rem(me_row + n_row - 1 - d, n_row) == r
            term = jnp.where(is_it, row_in[d], 0.0 if term is None else term)
        term = acc[keep, :] if term is None else jnp.where(me_row == r, acc[keep, :], term)
        total = term if total is None else total + term
    gat[keep, :] = total
    pending += copies

    for index in reversed(range(len(stages))):
        size, mine, others = stages[index]
        start, piece, first = spans[index]
        own = pl.ds(pl.multiple_of(start + mine * piece, 8), piece)
        copies = []
        for d, (_, target) in enumerate(others):
            copy = pltpu.make_async_remote_copy(
                src_ref=gat.at[own],
                dst_ref=gat.at[own],
                send_sem=send_g.at[first + d],
                recv_sem=recv_g.at[first + d],
                device_id={"col": target},
                device_id_type=MESH,
            )
            copy.start()
            copies.append(copy)
        if index == len(stages) - 1:
            finish_cols()
            peak = jnp.max(jnp.sum(probe[0] * probe[0] + probe[1] * probe[1], axis=0))
            change = ext_out[...] / peak
            if kind == "all":
                rows_at = lax.broadcasted_iota(jnp.int32, (full_rows, full_cols), 0)
                cols_at = lax.broadcasted_iota(jnp.int32, (full_rows, full_cols), 1)
                first_row = jnp.where(me_row == 0, rim, 0)
                last_row = jnp.where(me_row == n_row - 1, full_rows - rim, full_rows)
                first_col = jnp.where(me_col == 0, rim, 0)
                last_col = jnp.where(me_col == n_col - 1, full_cols - rim, full_cols)
                inside = (rows_at >= first_row) & (rows_at < last_row)
                inside = inside & (cols_at >= first_col) & (cols_at < last_col)
                change = jnp.where(inside[None], change, 0.0)
            ext_out[...] = ext[...] + change
        for d, (q, target) in enumerate(others):
            sender = lax.rem(mine + size - 1 - d, size)
            place = gat.at[pl.ds(pl.multiple_of(start + sender * piece, 8), piece)]
            pltpu.make_async_remote_copy(
                src_ref=place,
                dst_ref=place,
                send_sem=send_g.at[first + d],
                recv_sem=recv_g.at[first + d],
                device_id={"col": target},
                device_id_type=MESH,
            ).wait_recv()
        pending += copies

    weight = gat[pl.ds(2 * modes * pix, pix), :]
    for k in range(2):
        for m in range(modes):
            probe_out[k, m] = gat[pl.ds((k * modes + m) * pix, pix), :] / weight
    for copy in pending:
        copy.wait_send()
    row_edges.drain()
    col_edges.drain()


def exchange(kind, ident, upd, rim, ext=None, probe=None, sums=None):
    full_rows, full_cols = upd.shape[1], upd.shape[2]
    wide = 2 * rim
    row_width = wide if kind == "all" else rim
    height = full_rows - wide if kind == "tile" else full_rows
    n_row, n_col = lax.axis_size("row"), lax.axis_size("col")
    scratch = [
        pltpu.VMEM(upd.shape, jnp.float32),
        pltpu.VMEM((2, row_width, full_cols), jnp.float32),
        pltpu.VMEM((2, row_width, full_cols), jnp.float32),
        pltpu.VMEM((2, height, wide), jnp.float32),
        pltpu.VMEM((2, height, wide), jnp.float32),
        pltpu.SemaphoreType.DMA((2, 2)),
        pltpu.SemaphoreType.DMA((2, 2)),
    ]
    out = jax.ShapeDtypeStruct(upd.shape, jnp.float32)
    modes = pix = 0
    if kind == "rim":
        operands, outs = [upd], (out,)
    else:
        modes, pix = probe.shape[1], probe.shape[2]
        operands = [upd, ext, probe, sums]
        outs = (out, jax.ShapeDtypeStruct(probe.shape, jnp.float32))
        rows = sums.shape[0] * pix
        factors = col_factors(n_col)
        hops = sum(f - 1 for f in factors)
        scratch += [
            pltpu.VMEM((rows, pix), jnp.float32),
            pltpu.VMEM((rows, pix), jnp.float32),
            pltpu.VMEM((max(n_row - 1, 1), rows // n_col, pix), jnp.float32),
        ]
        scratch += [pltpu.SemaphoreType.DMA((hops,))] * 4
        scratch += [pltpu.SemaphoreType.DMA((max(n_row - 1, 1),))] * 2
        length = rows
        for f in factors:
            length //= f
            scratch.append(pltpu.VMEM((f - 1, length, pix), jnp.float32))
    return pl.pallas_call(
        functools.partial(exchange_kernel, kind, rim, modes, pix),
        out_shape=outs,
        in_specs=[VMEM] * len(operands),
        out_specs=tuple([VMEM] * len(outs)),
        scratch_shapes=scratch,
        compiler_params=pltpu.CompilerParams(
            collective_id=ident, has_side_effects=True, vmem_limit_bytes=LIMIT
        ),
        name="exchange_" + kind,
    )(*operands)


def on_device(object_field, probe, patterns, row_scales, positions, counts):
    modes, pix = probe.shape[1], probe.shape[2]
    rim = pix // 2
    tables = [jnp.asarray(t) for t in dft_tables(pix)]
    amp = patterns[0, 0].astype(jnp.float32) * row_scales[0, 0][..., None]
    starts = positions[0, 0]
    step = math.lcm(8 * lax.axis_size("col"), pix)
    rows_padded = -(-(2 * modes + 1) * pix // step) * step
    padded = jnp.pad(object_field, ((0, 0), (rim, rim), (rim, rim)))
    (ext,) = exchange("rim", 0, padded, rim)
    for pass_number in range(PASSES):
        upd, sums = run_pass(ext, probe, amp, starts, counts, tables, rows_padded)
        kind = "tile" if pass_number == PASSES - 1 else "all"
        ext, probe = exchange(kind, pass_number + 1, upd, rim, ext, probe, sums)
    return (ext[:, rim:-rim, rim:-rim], probe)


def solution(mesh):
    placed = (
        P(None, "row", "col"),
        P(),
        P("row", "col", None, None, None),
        P("row", "col", None, None),
        P("row", "col", None, None),
        P("row", "col"),
    )
    return jax.shard_map(
        on_device,
        mesh=mesh,
        in_specs=placed,
        out_specs=(P(None, "row", "col"), P()),
        check_vma=False,
    )
```

```python
import functools
import math

import jax
import jax.numpy as jnp
import numpy as np
from jax import lax
from jax.experimental import pallas as pl
from jax.experimental.pallas import tpu as pltpu
from jax.sharding import PartitionSpec as P

PASSES = 2
TOGETHER = 2
MESH = pl.DeviceIdType.MESH
VMEM = pl.BlockSpec(memory_space=pltpu.VMEM)
SMEM = pl.BlockSpec(memory_space=pltpu.SMEM)
LIMIT = 48 * 1024 * 1024


def dft_tables(length):
    index = np.arange(length)
    angle = (index[:, None] * index[None, :] % length) * (2.0 * math.pi / length)
    cosine, sine = np.cos(angle), np.sin(angle)
    forward = np.block([[cosine, -sine], [sine, cosine]]).astype(np.float32)
    inverse = np.block([[cosine, sine], [-sine, cosine]]).astype(np.float32)
    rights, lefts = [], []
    for table in (forward, inverse):
        high = table.astype(jnp.bfloat16)
        low = (table - high.astype(np.float32)).astype(jnp.bfloat16)
        rights.append(np.concatenate([high, high, low], 0))
        lefts.append(np.concatenate([high, high, low], 1))
    return rights + lefts


def split(value, axis):
    high = value.astype(jnp.bfloat16)
    low = (value - high.astype(jnp.float32)).astype(jnp.bfloat16)
    return jnp.concatenate([high, low, high], axis)


def times_table(value, table):
    return jnp.dot(split(value, 1), table[...], preferred_element_type=jnp.float32)


def table_times(table, value):
    return jnp.dot(table[...], split(value, 0), preferred_element_type=jnp.float32)


def pass_kernel(
    pos, count, ext, probe, amp, fwd_right, inv_right, fwd_left, inv_left, upd, sums, power, far, wave
):
    modes, pix = probe.shape[1], probe.shape[2]
    group = 2 if modes % 2 == 0 else 1
    firsts = range(0, modes, group)
    together = wave.shape[0]
    last = pos.shape[0] - 1
    tall = pix + 8
    upd[...] = jnp.zeros_like(upd)
    sums[...] = jnp.zeros_like(sums)
    power[...] = jnp.sum(probe[0] * probe[0] + probe[1] * probe[1], axis=0)

    def body(step, carry):
        at = [jnp.minimum(step * together + k, last) for k in range(together)]
        places = []
        for k, p in enumerate(at):
            row, col = pos[p, 0], pos[p, 1]
            shift, down = lax.rem(col, pix), lax.rem(row, 8)
            rows = pl.ds(pl.multiple_of(row // 8 * 8, 8), tall)
            lanes = pl.ds(pl.multiple_of(col // pix * pix, pix), 2 * pix)
            places.append((rows, lanes, shift, down))
            live = jnp.where(step * together + k < count[0, 0], 1.0, 0.0).astype(jnp.float32)
            for plane in range(2):
                moved = pltpu.roll(ext[plane, rows, lanes], lax.rem(2 * pix - shift, 2 * pix), 1)
                moved = pltpu.roll(moved[:, :pix], lax.rem(tall - down, tall), 0)[:pix]
                wave[k, plane] = moved * live
        halves, intensity = {}, [None] * together
        for first in firsts:
            for k in range(together):
                o_re, o_im = wave[k, 0], wave[k, 1]
                exits = []
                for m in range(first, first + group):
                    p_re, p_im = probe[0, m], probe[1, m]
                    exits.append(
                        jnp.concatenate([p_re * o_re - p_im * o_im, p_re * o_im + p_im * o_re], 1)
                    )
                halves[k, first] = times_table(jnp.concatenate(exits, 0), fwd_right)
        for first in firsts:
            for k in range(together):
                parts = [halves[k, first][j * pix : (j + 1) * pix] for j in range(group)]
                stacked = jnp.concatenate(
                    [jnp.concatenate([x[:, :pix], x[:, pix:]], 0) for x in parts], 1
                )
                full = table_times(inv_left, stacked)
                far[k, :, first * pix : (first + group) * pix] = full
                for j in range(group):
                    block = full[:, j * pix : (j + 1) * pix]
                    term = block[:pix] * block[:pix] + block[pix:] * block[pix:]
                    intensity[k] = term if intensity[k] is None else intensity[k] + term
        factors = []
        for k, p in enumerate(at):
            size = jnp.maximum(jnp.sqrt(intensity[k]) * (1.0 / pix), 0.5)
            factors.append(amp[p] / size * (1.0 / (pix * pix)))
        for first in firsts:
            for k in range(together):
                both = jnp.concatenate([factors[k]] * 2, 0)
                scaled = far[k, :, first * pix : (first + group) * pix]
                scaled = scaled * jnp.concatenate([both] * group, 1)
                halves[k, first] = table_times(fwd_left, scaled)
        change = [None] * together
        for first in firsts:
            grown = [None] * (2 * group)
            for k in range(together):
                o_re, o_im = wave[k, 0], wave[k, 1]
                parts = [halves[k, first][:, j * pix : (j + 1) * pix] for j in range(group)]
                flat = jnp.concatenate(
                    [jnp.concatenate([x[:pix], x[pix:]], 1) for x in parts], 0
                )
                back = times_table(flat, inv_right)
                if change[k] is None:
                    change[k] = [-power[...] * o_re, -power[...] * o_im]
                for j in range(group):
                    b_re = back[j * pix : (j + 1) * pix, :pix]
                    b_im = back[j * pix : (j + 1) * pix, pix:]
                    p_re, p_im = probe[0, first + j], probe[1, first + j]
                    change[k][0] += p_re * b_re + p_im * b_im
                    change[k][1] += p_re * b_im - p_im * b_re
                    for part, term in (
                        (2 * j, o_re * b_re + o_im * b_im),
                        (2 * j + 1, o_re * b_im - o_im * b_re),
                    ):
                        grown[part] = term if grown[part] is None else grown[part] + term
            for j in range(group):
                sums[first + j] += grown[2 * j]
                sums[modes + first + j] += grown[2 * j + 1]
        sums[2 * modes] += sum(
            wave[k, 0] * wave[k, 0] + wave[k, 1] * wave[k, 1] for k in range(together)
        )
        for k, (rows, lanes, shift, down) in enumerate(places):
            for plane in range(2):
                moved = jnp.concatenate([change[k][plane], jnp.zeros((8, pix), jnp.float32)], 0)
                moved = pltpu.roll(moved, down, 0)
                moved = jnp.concatenate([moved, jnp.zeros_like(moved)], 1)
                upd[plane, rows, lanes] += pltpu.roll(moved, shift, 1)
        return carry

    lax.fori_loop(0, (count[0, 0] + together - 1) // together, body, 0)


def run_pass(ext, probe, amp, starts, counts, tables, rows_padded):
    modes, pix = probe.shape[1], probe.shape[2]
    planes = rows_padded // pix
    return pl.pallas_call(
        pass_kernel,
        out_shape=(
            jax.ShapeDtypeStruct(ext.shape, jnp.float32),
            jax.ShapeDtypeStruct((planes, pix, pix), jnp.float32),
        ),
        in_specs=[SMEM, SMEM] + [VMEM] * 7,
        out_specs=(VMEM, VMEM),
        scratch_shapes=[
            pltpu.VMEM((pix, pix), jnp.float32),
            pltpu.VMEM((TOGETHER, 2 * pix, modes * pix), jnp.float32),
            pltpu.VMEM((TOGETHER, 2, pix, pix), jnp.float32),
        ],
        compiler_params=pltpu.CompilerParams(vmem_limit_bytes=LIMIT),
        name="scan_pass",
    )(starts, counts, ext, probe, amp, *tables)


def col_factors(count):
    core = math.gcd(2, count)
    far = math.gcd(4, count // core)
    return [f for f in (core, count // core // far, far) if f > 1]


class Edges:
    def __init__(self, axis, send_sem, recv_sem):
        self.axis = axis
        self.count = lax.axis_size(axis)
        self.me = lax.axis_index(axis)
        self.has_low = self.me > 0
        self.has_high = self.me < self.count - 1
        self.sems = (send_sem, recv_sem)

    def greet(self, barrier):
        @pl.when(self.has_low)
        def _():
            pl.semaphore_signal(
                barrier, inc=1, device_id={self.axis: self.me - 1}, device_id_type=MESH
            )

        @pl.when(self.has_high)
        def _():
            pl.semaphore_signal(
                barrier, inc=1, device_id={self.axis: self.me + 1}, device_id_type=MESH
            )

        return self.has_low.astype(jnp.int32) + self.has_high.astype(jnp.int32)

    def copies(self, low_src, high_src, from_low, from_high):
        send, recv = self.sems

        def make(src, dst, slot, target):
            return pltpu.make_async_remote_copy(
                src_ref=src,
                dst_ref=dst,
                send_sem=send.at[slot],
                recv_sem=recv.at[slot],
                device_id={self.axis: target},
                device_id_type=MESH,
            )

        self.up = make(high_src, from_low, 0, self.me + 1)
        self.down = make(low_src, from_high, 1, self.me - 1)

    def start(self):
        @pl.when(self.has_high)
        def _():
            self.up.start()

        @pl.when(self.has_low)
        def _():
            self.down.start()

    def finish(self, add_low, add_high):
        @pl.when(self.has_low)
        def _():
            self.up.wait_recv()
            add_low()

        @pl.when(self.has_high)
        def _():
            self.down.wait_recv()
            add_high()

    def drain(self):
        @pl.when(self.has_high)
        def _():
            self.up.wait_send()

        @pl.when(self.has_low)
        def _():
            self.down.wait_send()


def exchange_kernel(
    kind, rim, modes, pix, *refs
):
    reduce = kind != "rim"
    if reduce:
        (upd, ext, probe, sums, ext_out, probe_out) = refs[:6]
        scratch = refs[6:]
    else:
        upd, ext_out = refs[:2]
        scratch = refs[2:]
    work, low_r, high_r, low_c, high_c, send_e, recv_e = scratch[:7]
    full_rows, full_cols = work.shape[1], work.shape[2]
    row_edges = Edges("row", send_e.at[0], recv_e.at[0])
    col_edges = Edges("col", send_e.at[1], recv_e.at[1])
    wide = 2 * rim
    if kind == "rim":
        send_high, send_low = (full_rows - wide, rim), (rim, rim)
        put_low, put_high = (0, rim), (full_rows - rim, rim)
    elif kind == "all":
        send_high, send_low = (full_rows - wide, wide), (0, wide)
        put_low, put_high = (0, wide), (full_rows - wide, wide)
    else:
        send_high, send_low = (full_rows - rim, rim), (0, rim)
        put_low, put_high = (rim, rim), (full_rows - wide, rim)
    row_span = (rim, full_rows - wide) if kind == "tile" else (0, full_rows)

    barrier = pltpu.get_barrier_semaphore()
    greeted = row_edges.greet(barrier) + col_edges.greet(barrier)
    n_row, n_col = lax.axis_size("row"), lax.axis_size("col")
    me_row, me_col = lax.axis_index("row"), lax.axis_index("col")
    stages = []
    if reduce:
        stride = 1
        for size in col_factors(n_col):
            mine = lax.rem(me_col // stride, size)
            base = me_col - mine * stride
            others = [lax.rem(mine + d, size) for d in range(1, size)]
            stages.append((size, mine, [(q, base + q * stride) for q in others]))
            stride *= size
        row_others = [lax.rem(me_row + d, n_row) for d in range(1, n_row)]
        for _, _, others in stages:
            for _, target in others:
                pl.semaphore_signal(barrier, inc=1, device_id={"col": target}, device_id_type=MESH)
        for target in row_others:
            pl.semaphore_signal(barrier, inc=1, device_id={"row": target}, device_id_type=MESH)
        greeted = greeted + sum(len(s[2]) for s in stages) + len(row_others)
    pl.semaphore_wait(barrier, greeted)

    row_edges.copies(
        upd.at[:, pl.ds(*send_low), :], upd.at[:, pl.ds(*send_high), :], low_r, high_r
    )
    row_edges.start()

    def finish_rows():
        work[...] = upd[...]

        def add_low():
            work[:, pl.ds(*put_low), :] += low_r[...]

        def add_high():
            work[:, pl.ds(*put_high), :] += high_r[...]

        row_edges.finish(add_low, add_high)
        col_edges.copies(
            work.at[:, pl.ds(*row_span), pl.ds(0, wide)],
            work.at[:, pl.ds(*row_span), pl.ds(full_cols - wide, wide)],
            low_c,
            high_c,
        )
        col_edges.start()

    def finish_cols():
        ext_out[...] = work[...]

        def add_low():
            ext_out[:, pl.ds(*row_span), pl.ds(0, wide)] += low_c[...]

        def add_high():
            ext_out[:, pl.ds(*row_span), pl.ds(full_cols - wide, wide)] += high_c[...]

        col_edges.finish(add_low, add_high)

    if not reduce:
        finish_rows()
        finish_cols()
        row_edges.drain()
        col_edges.drain()
        return

    acc, gat, row_in, send_s, recv_s, send_g, recv_g, send_x, recv_x = scratch[7:16]
    landings = scratch[16:]
    pending = []
    offset, length, slot = 0, acc.shape[0], 0
    acc[...] = sums[...].reshape(acc.shape)
    spans = []
    for index, (size, mine, others) in enumerate(stages):
        piece = length // size
        spans.append((offset, piece, slot))
        copies = []
        for d, (q, target) in enumerate(others):
            copy = pltpu.make_async_remote_copy(
                src_ref=acc.at[pl.ds(pl.multiple_of(offset + q * piece, 8), piece)],
                dst_ref=landings[index].at[d],
                send_sem=send_s.at[slot],
                recv_sem=recv_s.at[slot],
                device_id={"col": target},
                device_id_type=MESH,
            )
            slot += 1
            copy.start()
            copies.append(copy)
        if index == 1 or len(stages) == 1:
            finish_rows()
        keep = pl.ds(pl.multiple_of(offset + mine * piece, 8), piece)
        total = acc[keep, :]
        for d, copy in enumerate(copies):
            copy.wait_recv()
            total = total + landings[index][d]
        acc[keep, :] = total
        pending += copies
        offset, length = offset + mine * piece, piece

    keep = pl.ds(pl.multiple_of(offset, 8), length)
    copies = []
    for d, target in enumerate(row_others):
        copy = pltpu.make_async_remote_copy(
            src_ref=acc.at[keep],
            dst_ref=row_in.at[d],
            send_sem=send_x.at[d],
            recv_sem=recv_x.at[d],
            device_id={"row": target},
            device_id_type=MESH,
        )
        copy.start()
        copies.append(copy)
    for copy in copies:
        copy.wait_recv()
    total = None
    for r in range(n_row):
        term = None
        for d in range(n_row - 1):
            is_it = lax.rem(me_row + n_row - 1 - d, n_row) == r
            term = jnp.where(is_it, row_in[d], 0.0 if term is None else term)
        term = acc[keep, :] if term is None else jnp.where(me_row == r, acc[keep, :], term)
        total = term if total is None else total + term
    gat[keep, :] = total
    pending += copies

    for index in reversed(range(len(stages))):
        size, mine, others = stages[index]
        start, piece, first = spans[index]
        own = pl.ds(pl.multiple_of(start + mine * piece, 8), piece)
        copies = []
        for d, (_, target) in enumerate(others):
            copy = pltpu.make_async_remote_copy(
                src_ref=gat.at[own],
                dst_ref=gat.at[own],
                send_sem=send_g.at[first + d],
                recv_sem=recv_g.at[first + d],
                device_id={"col": target},
                device_id_type=MESH,
            )
            copy.start()
            copies.append(copy)
        if index == len(stages) - 1:
            finish_cols()
            peak = jnp.max(jnp.sum(probe[0] * probe[0] + probe[1] * probe[1], axis=0))
            change = ext_out[...] / peak
            if kind == "all":
                rows_at = lax.broadcasted_iota(jnp.int32, (full_rows, full_cols), 0)
                cols_at = lax.broadcasted_iota(jnp.int32, (full_rows, full_cols), 1)
                first_row = jnp.where(me_row == 0, rim, 0)
                last_row = jnp.where(me_row == n_row - 1, full_rows - rim, full_rows)
                first_col = jnp.where(me_col == 0, rim, 0)
                last_col = jnp.where(me_col == n_col - 1, full_cols - rim, full_cols)
                inside = (rows_at >= first_row) & (rows_at < last_row)
                inside = inside & (cols_at >= first_col) & (cols_at < last_col)
                change = jnp.where(inside[None], change, 0.0)
            ext_out[...] = ext[...] + change
        for d, (q, target) in enumerate(others):
            sender = lax.rem(mine + size - 1 - d, size)
            place = gat.at[pl.ds(pl.multiple_of(start + sender * piece, 8), piece)]
            pltpu.make_async_remote_copy(
                src_ref=place,
                dst_ref=place,
                send_sem=send_g.at[first + d],
                recv_sem=recv_g.at[first + d],
                device_id={"col": target},
                device_id_type=MESH,
            ).wait_recv()
        pending += copies

    weight = gat[pl.ds(2 * modes * pix, pix), :]
    for k in range(2):
        for m in range(modes):
            probe_out[k, m] = gat[pl.ds((k * modes + m) * pix, pix), :] / weight
    for copy in pending:
        copy.wait_send()
    row_edges.drain()
    col_edges.drain()


def exchange(kind, ident, upd, rim, ext=None, probe=None, sums=None):
    full_rows, full_cols = upd.shape[1], upd.shape[2]
    wide = 2 * rim
    row_width = wide if kind == "all" else rim
    height = full_rows - wide if kind == "tile" else full_rows
    n_row, n_col = lax.axis_size("row"), lax.axis_size("col")
    scratch = [
        pltpu.VMEM(upd.shape, jnp.float32),
        pltpu.VMEM((2, row_width, full_cols), jnp.float32),
        pltpu.VMEM((2, row_width, full_cols), jnp.float32),
        pltpu.VMEM((2, height, wide), jnp.float32),
        pltpu.VMEM((2, height, wide), jnp.float32),
        pltpu.SemaphoreType.DMA((2, 2)),
        pltpu.SemaphoreType.DMA((2, 2)),
    ]
    out = jax.ShapeDtypeStruct(upd.shape, jnp.float32)
    modes = pix = 0
    if kind == "rim":
        operands, outs = [upd], (out,)
    else:
        modes, pix = probe.shape[1], probe.shape[2]
        operands = [upd, ext, probe, sums]
        outs = (out, jax.ShapeDtypeStruct(probe.shape, jnp.float32))
        rows = sums.shape[0] * pix
        factors = col_factors(n_col)
        hops = sum(f - 1 for f in factors)
        scratch += [
            pltpu.VMEM((rows, pix), jnp.float32),
            pltpu.VMEM((rows, pix), jnp.float32),
            pltpu.VMEM((max(n_row - 1, 1), rows // n_col, pix), jnp.float32),
        ]
        scratch += [pltpu.SemaphoreType.DMA((hops,))] * 4
        scratch += [pltpu.SemaphoreType.DMA((max(n_row - 1, 1),))] * 2
        length = rows
        for f in factors:
            length //= f
            scratch.append(pltpu.VMEM((f - 1, length, pix), jnp.float32))
    return pl.pallas_call(
        functools.partial(exchange_kernel, kind, rim, modes, pix),
        out_shape=outs,
        in_specs=[VMEM] * len(operands),
        out_specs=tuple([VMEM] * len(outs)),
        scratch_shapes=scratch,
        compiler_params=pltpu.CompilerParams(
            collective_id=ident, has_side_effects=True, vmem_limit_bytes=LIMIT
        ),
        name="exchange_" + kind,
    )(*operands)


def on_device(object_field, probe, patterns, row_scales, positions, counts):
    modes, pix = probe.shape[1], probe.shape[2]
    rim = pix // 2
    tables = [jnp.asarray(t) for t in dft_tables(pix)]
    amp = patterns[0, 0].astype(jnp.float32) * row_scales[0, 0][..., None]
    starts = positions[0, 0]
    step = math.lcm(8 * lax.axis_size("col"), pix)
    rows_padded = -(-(2 * modes + 1) * pix // step) * step
    padded = jnp.pad(object_field, ((0, 0), (rim, rim), (rim, rim)))
    (ext,) = exchange("rim", 0, padded, rim)
    for pass_number in range(PASSES):
        upd, sums = run_pass(ext, probe, amp, starts, counts, tables, rows_padded)
        kind = "tile" if pass_number == PASSES - 1 else "all"
        ext, probe = exchange(kind, pass_number + 1, upd, rim, ext, probe, sums)
    return (ext[:, rim:-rim, rim:-rim], probe)


def solution(mesh):
    placed = (
        P(None, "row", "col"),
        P(),
        P("row", "col", None, None, None),
        P("row", "col", None, None),
        P("row", "col", None, None),
        P("row", "col"),
    )
    return jax.shard_map(
        on_device,
        mesh=mesh,
        in_specs=placed,
        out_specs=(P(None, "row", "col"), P()),
        check_vma=False,
    )
```

```python
import functools
import math

import jax
import jax.numpy as jnp
import numpy as np
from jax import lax
from jax.experimental import pallas as pl
from jax.experimental.pallas import tpu as pltpu
from jax.sharding import PartitionSpec as P

PASSES = 2
TOGETHER = 2
MESH = pl.DeviceIdType.MESH
VMEM = pl.BlockSpec(memory_space=pltpu.VMEM)
SMEM = pl.BlockSpec(memory_space=pltpu.SMEM)
LIMIT = 48 * 1024 * 1024


def dft_tables(length):
    index = np.arange(length)
    angle = (index[:, None] * index[None, :] % length) * (2.0 * math.pi / length)
    cosine, sine = np.cos(angle), np.sin(angle)
    forward = np.block([[cosine, -sine], [sine, cosine]]).astype(np.float32)
    inverse = np.block([[cosine, sine], [-sine, cosine]]).astype(np.float32)
    rights, lefts = [], []
    for table in (forward, inverse):
        high = table.astype(jnp.bfloat16)
        low = (table - high.astype(np.float32)).astype(jnp.bfloat16)
        rights.append(np.concatenate([high, high, low], 0))
        lefts.append(np.concatenate([high, high, low], 1))
    return rights + lefts


def split(value, axis):
    high = value.astype(jnp.bfloat16)
    low = (value - high.astype(jnp.float32)).astype(jnp.bfloat16)
    return jnp.concatenate([high, low, high], axis)


def times_table(value, table):
    return jnp.dot(split(value, 1), table[...], preferred_element_type=jnp.float32)


def table_times(table, value):
    return jnp.dot(table[...], split(value, 0), preferred_element_type=jnp.float32)


def pass_kernel(
    pos, count, ext, probe, amp, fwd_right, inv_right, fwd_left, inv_left, upd, sums, power, far, wave
):
    modes, pix = probe.shape[1], probe.shape[2]
    group = 2 if modes % 2 == 0 else 1
    firsts = range(0, modes, group)
    together = wave.shape[0]
    last = pos.shape[0] - 1
    tall = pix + 8
    upd[...] = jnp.zeros_like(upd)
    sums[...] = jnp.zeros_like(sums)
    power[...] = jnp.sum(probe[0] * probe[0] + probe[1] * probe[1], axis=0)

    def body(step, carry):
        at = [jnp.minimum(step * together + k, last) for k in range(together)]
        places = []
        for k, p in enumerate(at):
            row, col = pos[p, 0], pos[p, 1]
            shift, down = lax.rem(col, pix), lax.rem(row, 8)
            rows = pl.ds(pl.multiple_of(row // 8 * 8, 8), tall)
            lanes = pl.ds(pl.multiple_of(col // pix * pix, pix), 2 * pix)
            places.append((rows, lanes, shift, down))
            live = jnp.where(step * together + k < count[0, 0], 1.0, 0.0).astype(jnp.float32)
            for plane in range(2):
                moved = pltpu.roll(ext[plane, rows, lanes], lax.rem(2 * pix - shift, 2 * pix), 1)
                moved = pltpu.roll(moved[:, :pix], lax.rem(tall - down, tall), 0)[:pix]
                wave[k, plane] = moved * live
        halves, intensity = {}, [None] * together
        for first in firsts:
            for k in range(together):
                o_re, o_im = wave[k, 0], wave[k, 1]
                exits = []
                for m in range(first, first + group):
                    p_re, p_im = probe[0, m], probe[1, m]
                    exits.append(
                        jnp.concatenate([p_re * o_re - p_im * o_im, p_re * o_im + p_im * o_re], 1)
                    )
                halves[k, first] = times_table(jnp.concatenate(exits, 0), fwd_right)
        for first in firsts:
            for k in range(together):
                parts = [halves[k, first][j * pix : (j + 1) * pix] for j in range(group)]
                stacked = jnp.concatenate(
                    [jnp.concatenate([x[:, :pix], x[:, pix:]], 0) for x in parts], 1
                )
                full = table_times(inv_left, stacked)
                far[k, :, first * pix : (first + group) * pix] = full
                for j in range(group):
                    block = full[:, j * pix : (j + 1) * pix]
                    term = block[:pix] * block[:pix] + block[pix:] * block[pix:]
                    intensity[k] = term if intensity[k] is None else intensity[k] + term
        factors = []
        for k, p in enumerate(at):
            size = jnp.maximum(jnp.sqrt(intensity[k]) * (1.0 / pix), 0.5)
            factors.append(amp[p] / size * (1.0 / (pix * pix)))
        for first in firsts:
            for k in range(together):
                both = jnp.concatenate([factors[k]] * 2, 0)
                scaled = far[k, :, first * pix : (first + group) * pix]
                scaled = scaled * jnp.concatenate([both] * group, 1)
                halves[k, first] = table_times(fwd_left, scaled)
        change = [None] * together
        for first in firsts:
            grown = [None] * (2 * group)
            for k in range(together):
                o_re, o_im = wave[k, 0], wave[k, 1]
                parts = [halves[k, first][:, j * pix : (j + 1) * pix] for j in range(group)]
                flat = jnp.concatenate(
                    [jnp.concatenate([x[:pix], x[pix:]], 1) for x in parts], 0
                )
                back = times_table(flat, inv_right)
                if change[k] is None:
                    change[k] = [-power[...] * o_re, -power[...] * o_im]
                for j in range(group):
                    b_re = back[j * pix : (j + 1) * pix, :pix]
                    b_im = back[j * pix : (j + 1) * pix, pix:]
                    p_re, p_im = probe[0, first + j], probe[1, first + j]
                    change[k][0] += p_re * b_re + p_im * b_im
                    change[k][1] += p_re * b_im - p_im * b_re
                    for part, term in (
                        (2 * j, o_re * b_re + o_im * b_im),
                        (2 * j + 1, o_re * b_im - o_im * b_re),
                    ):
                        grown[part] = term if grown[part] is None else grown[part] + term
            for j in range(group):
                sums[first + j] += grown[2 * j]
                sums[modes + first + j] += grown[2 * j + 1]
        sums[2 * modes] += sum(
            wave[k, 0] * wave[k, 0] + wave[k, 1] * wave[k, 1] for k in range(together)
        )
        for k, (rows, lanes, shift, down) in enumerate(places):
            for plane in range(2):
                moved = jnp.concatenate([change[k][plane], jnp.zeros((8, pix), jnp.float32)], 0)
                moved = pltpu.roll(moved, down, 0)
                moved = jnp.concatenate([moved, jnp.zeros_like(moved)], 1)
                upd[plane, rows, lanes] += pltpu.roll(moved, shift, 1)
        return carry

    lax.fori_loop(0, (count[0, 0] + together - 1) // together, body, 0)


def run_pass(ext, probe, amp, starts, counts, tables, rows_padded):
    modes, pix = probe.shape[1], probe.shape[2]
    planes = rows_padded // pix
    return pl.pallas_call(
        pass_kernel,
        out_shape=(
            jax.ShapeDtypeStruct(ext.shape, jnp.float32),
            jax.ShapeDtypeStruct((planes, pix, pix), jnp.float32),
        ),
        in_specs=[SMEM, SMEM] + [VMEM] * 7,
        out_specs=(VMEM, VMEM),
        scratch_shapes=[
            pltpu.VMEM((pix, pix), jnp.float32),
            pltpu.VMEM((TOGETHER, 2 * pix, modes * pix), jnp.float32),
            pltpu.VMEM((TOGETHER, 2, pix, pix), jnp.float32),
        ],
        compiler_params=pltpu.CompilerParams(vmem_limit_bytes=LIMIT),
        name="scan_pass",
    )(starts, counts, ext, probe, amp, *tables)


def col_factors(n_row, n_col):
    core = math.gcd(2, n_col)
    far = math.gcd(4, n_col // core)
    return core, n_row * (n_col // core // far), far


def half_pack(re, im, upper):
    width = re.shape[-1]
    lane = lax.broadcasted_iota(jnp.int32, re.shape, 1)
    if upper:
        return jnp.where(lane < width // 2, pltpu.roll(re, width // 2, 1), im)
    return jnp.where(lane < width // 2, re, pltpu.roll(im, width // 2, 1))


def half_unpack(packed, upper):
    width = packed.shape[-1]
    lane = lax.broadcasted_iota(jnp.int32, packed.shape, 1)
    turned = pltpu.roll(packed, width // 2, 1)
    if upper:
        inside = lane >= width // 2
        return jnp.where(inside, turned, 0.0), jnp.where(inside, packed, 0.0)
    inside = lane < width // 2
    return jnp.where(inside, packed, 0.0), jnp.where(inside, turned, 0.0)


def exchange_kernel(kind, rim, modes, pix, *refs):
    reduce = kind != "rim"
    if reduce:
        (upd, ext, probe, sums, ext_out, probe_out) = refs[:6]
        scratch = refs[6:]
    else:
        (field, patterns, scales, ext_out, amp) = refs[:5]
        scratch = refs[5:]
    work, low_r, high_r, low_c, high_c, low_s, high_s, send_r, recv_r, send_c, recv_c = scratch[:11]
    full_rows, full_cols = work.shape[1], work.shape[2]
    wide = 2 * rim
    packed = kind != "all"
    if kind == "rim":
        send_high, send_low = (full_rows - wide, rim), (rim, rim)
        put_low, put_high = (0, rim), (full_rows - rim, rim)
    elif kind == "all":
        send_high, send_low = (full_rows - wide, wide), (0, wide)
        put_low, put_high = (0, wide), (full_rows - wide, wide)
    else:
        send_high, send_low = (full_rows - rim, rim), (0, rim)
        put_low, put_high = (rim, rim), (full_rows - wide, rim)
    put_middle = (sum(put_low), put_high[0] - sum(put_low))
    top = put_low[0]
    blocks = [put_low, put_middle, put_high]
    n_row, n_col = lax.axis_size("row"), lax.axis_size("col")
    me_row, me_col = lax.axis_index("row"), lax.axis_index("col")
    row_low, row_high = me_row > 0, me_row < n_row - 1
    col_low, col_high = me_col > 0, me_col < n_col - 1

    barrier = pltpu.get_barrier_semaphore()

    def greet(target):
        pl.semaphore_signal(barrier, inc=1, device_id=target, device_id_type=MESH)

    pl.when(row_low)(lambda: greet({"row": me_row - 1}))
    pl.when(row_high)(lambda: greet({"row": me_row + 1}))
    pl.when(col_low)(lambda: greet({"col": me_col - 1}))
    pl.when(col_high)(lambda: greet({"col": me_col + 1}))
    greeted = sum(x.astype(jnp.int32) for x in (row_low, row_high, col_low, col_high))
    stages = []
    if reduce:
        core, plane, far = col_factors(n_row, n_col)
        near = plane // n_row
        c = lax.rem(me_col, core)
        y = lax.rem(lax.div(me_col, core), near)
        z = lax.div(me_col, core * near)

        def in_core(q):
            return me_row, me_col + q - c

        def in_plane(q):
            return lax.div(q, near), me_col + (lax.rem(q, near) - y) * core

        def across(q):
            return me_row, me_col + (q - z) * (near * core)

        mine_plane, mine_far = me_row * near + y, z
        orders = [(plane, mine_plane, in_plane), (far, mine_far, across)]
        if plane == far and core == 2:
            def pick(first, second):
                return jnp.where(c == 0, first, second)

            def begin(q):
                return tuple(pick(a, b) for a, b in zip(in_plane(q), across(q)))

            def end(q):
                return tuple(pick(a, b) for a, b in zip(across(q), in_plane(q)))

            orders = [
                (far, pick(mine_plane, mine_far), begin),
                (far, pick(mine_far, mine_plane), end),
            ]
        for size, mine, where in [(core, c, in_core)] + orders:
            others = []
            for d in range(1, size):
                q = lax.rem(mine + d, size)
                row, col = where(q)
                others.append((q, {"row": row, "col": col}))
            if others:
                stages.append((size, mine, others))
        for _, _, others in stages:
            for _, target in others:
                greet(target)
        greeted = greeted + sum(len(stage[2]) for stage in stages)

    if reduce:
        border = upd
    else:
        border = work
        blank = jnp.zeros((field.shape[1], wide), jnp.float32)
        work[...] = jnp.zeros_like(work)
        for k in range(2):
            work[k, rim:-rim, :] = pltpu.roll(jnp.concatenate([field[k], blank], 1), rim, 1)
    pl.semaphore_wait(barrier, greeted)

    def copy_to(src, dst, send, recv, target):
        return pltpu.make_async_remote_copy(
            src_ref=src,
            dst_ref=dst,
            send_sem=send,
            recv_sem=recv,
            device_id=target,
            device_id_type=MESH,
        )

    row_up = copy_to(
        border.at[:, pl.ds(*send_high), :], low_r, send_r.at[0], recv_r.at[0], {"row": me_row + 1}
    )
    row_down = copy_to(
        border.at[:, pl.ds(*send_low), :], high_r, send_r.at[1], recv_r.at[1], {"row": me_row - 1}
    )
    pl.when(row_high)(row_up.start)
    pl.when(row_low)(row_down.start)

    col_up, col_down = [], []
    for index, (start, length) in enumerate(blocks):
        at = pl.ds(start - top, length)
        if packed:
            sources = high_s.at[at, :], low_s.at[at, :]
            places = low_c.at[at, :], high_c.at[at, :]
        else:
            span = pl.ds(start, length)
            sources = work.at[:, span, pl.ds(full_cols - wide, wide)], work.at[:, span, pl.ds(0, wide)]
            places = low_c.at[:, at, :], high_c.at[:, at, :]
        sems = send_c.at[0, index], recv_c.at[0, index]
        col_up.append(copy_to(sources[0], places[0], *sems, {"col": me_col + 1}))
        sems = send_c.at[1, index], recv_c.at[1, index]
        col_down.append(copy_to(sources[1], places[1], *sems, {"col": me_col - 1}))

    def start_block(index):
        start, length = blocks[index]
        if packed:
            span, at = pl.ds(start, length), pl.ds(start - top, length)
            high, low = pl.ds(full_cols - wide, wide), pl.ds(0, wide)
            upper = kind == "tile"
            high_s[at, :] = half_pack(work[0, span, high], work[1, span, high], upper)
            low_s[at, :] = half_pack(work[0, span, low], work[1, span, low], not upper)
        pl.when(col_high)(col_up[index].start)
        pl.when(col_low)(col_down[index].start)

    def begin_cols():
        if reduce:
            work[...] = upd[...]
        start_block(1)
        pl.when(jnp.logical_not(row_low))(lambda: start_block(0))
        pl.when(jnp.logical_not(row_high))(lambda: start_block(2))

    def finish_rows():
        @pl.when(row_low)
        def _():
            row_up.wait_recv()
            work[:, pl.ds(*put_low), :] += low_r[...]
            start_block(0)

        @pl.when(row_high)
        def _():
            row_down.wait_recv()
            work[:, pl.ds(*put_high), :] += high_r[...]
            start_block(2)

    def finish_cols():
        ext_out[...] = work[...]
        span = pl.ds(top, sum(put_high) - top)

        def land(copies, buffer, start, upper):
            for copy in copies:
                copy.wait_recv()
            lanes = pl.ds(start, wide)
            if packed:
                re, im = half_unpack(buffer[...], upper)
                ext_out[0, span, lanes] += re
                ext_out[1, span, lanes] += im
            else:
                ext_out[:, span, lanes] += buffer[...]

        pl.when(col_low)(lambda: land(col_up, low_c, 0, kind == "tile"))
        pl.when(col_high)(lambda: land(col_down, high_c, full_cols - wide, kind != "tile"))

    def drain():
        pl.when(row_high)(row_up.wait_send)
        pl.when(row_low)(row_down.wait_send)
        for index in range(3):
            pl.when(col_high)(col_up[index].wait_send)
            pl.when(col_low)(col_down[index].wait_send)

    if not reduce:
        begin_cols()
        for p in range(amp.shape[0]):
            column = jnp.broadcast_to(scales[p : p + 1, :], (pix, pix)).T
            amp[p] = patterns[p].astype(jnp.float32) * column
        finish_rows()
        finish_cols()
        drain()
        return

    acc, gat, send_s, recv_s, send_g, recv_g = scratch[11:17]
    landings = scratch[17:]
    pending = []
    offset, length, slot = 0, acc.shape[0], 0
    acc[...] = sums[...].reshape(acc.shape)
    spans = []
    for index, (size, mine, others) in enumerate(stages):
        piece = length // size
        spans.append((offset, piece, slot))
        copies = []
        for d, (q, target) in enumerate(others):
            copy = copy_to(
                acc.at[pl.ds(pl.multiple_of(offset + q * piece, 8), piece)],
                landings[index].at[d],
                send_s.at[slot],
                recv_s.at[slot],
                target,
            )
            slot += 1
            copy.start()
            copies.append(copy)
        if index == 0:
            begin_cols()
        keep = pl.ds(pl.multiple_of(offset + mine * piece, 8), piece)
        total = acc[keep, :]
        for d, copy in enumerate(copies):
            copy.wait_recv()
            total = total + landings[index][d]
        acc[keep, :] = total
        pending += copies
        offset, length = offset + mine * piece, piece

    keep = pl.ds(pl.multiple_of(offset, 8), length)
    gat[keep, :] = acc[keep, :]
    for index in reversed(range(len(stages))):
        size, mine, others = stages[index]
        start, piece, first = spans[index]
        own = pl.ds(pl.multiple_of(start + mine * piece, 8), piece)
        copies = []
        for d, (_, target) in enumerate(others):
            copy = copy_to(
                gat.at[own], gat.at[own], send_g.at[first + d], recv_g.at[first + d], target
            )
            copy.start()
            copies.append(copy)
        if index == len(stages) - 1:
            finish_rows()
        if index == 0:
            finish_cols()
            peak = jnp.max(jnp.sum(probe[0] * probe[0] + probe[1] * probe[1], axis=0))
            change = ext_out[...] / peak
            if kind == "all":
                rows_at = lax.broadcasted_iota(jnp.int32, (full_rows, full_cols), 0)
                cols_at = lax.broadcasted_iota(jnp.int32, (full_rows, full_cols), 1)
                first_row = jnp.where(me_row == 0, rim, 0)
                last_row = jnp.where(me_row == n_row - 1, full_rows - rim, full_rows)
                first_col = jnp.where(me_col == 0, rim, 0)
                last_col = jnp.where(me_col == n_col - 1, full_cols - rim, full_cols)
                inside = (rows_at >= first_row) & (rows_at < last_row)
                inside = inside & (cols_at >= first_col) & (cols_at < last_col)
                change = jnp.where(inside[None], change, 0.0)
            ext_out[...] = ext[...] + change
        for d in range(size - 1):
            sender = lax.rem(mine + size - 1 - d, size)
            place = gat.at[pl.ds(pl.multiple_of(start + sender * piece, 8), piece)]
            copy_to(place, place, send_g.at[first + d], recv_g.at[first + d], others[d][1]).wait_recv()
        pending += copies

    weight = gat[pl.ds(2 * modes * pix, pix), :]
    for k in range(2):
        for m in range(modes):
            probe_out[k, m] = gat[pl.ds((k * modes + m) * pix, pix), :] / weight
    for copy in pending:
        copy.wait_send()
    drain()


def exchange(kind, ident, shape, pix, operands):
    rim = pix // 2
    full_rows, full_cols = shape[1], shape[2]
    wide = 2 * rim
    row_width = wide if kind == "all" else rim
    height = full_rows - wide if kind == "tile" else full_rows
    n_row, n_col = lax.axis_size("row"), lax.axis_size("col")
    side = (2, height, wide) if kind == "all" else (height, wide)
    scratch = [
        pltpu.VMEM(shape, jnp.float32),
        pltpu.VMEM((2, row_width, full_cols), jnp.float32),
        pltpu.VMEM((2, row_width, full_cols), jnp.float32),
    ]
    scratch += [pltpu.VMEM(side, jnp.float32)] * 4
    scratch += [pltpu.SemaphoreType.DMA((2,))] * 2
    scratch += [pltpu.SemaphoreType.DMA((2, 3))] * 2
    out = jax.ShapeDtypeStruct(shape, jnp.float32)
    modes = 0
    if kind == "rim":
        outs = (out, jax.ShapeDtypeStruct(operands[1].shape, jnp.float32))
    else:
        probe, sums = operands[2:]
        modes = probe.shape[1]
        outs = (out, jax.ShapeDtypeStruct(probe.shape, jnp.float32))
        rows = sums.shape[0] * pix
        factors = [f for f in col_factors(n_row, n_col) if f > 1]
        hops = sum(f - 1 for f in factors)
        scratch += [pltpu.VMEM((rows, pix), jnp.float32)] * 2
        scratch += [pltpu.SemaphoreType.DMA((hops,))] * 4
        length = rows
        for f in factors:
            length //= f
            scratch.append(pltpu.VMEM((f - 1, length, pix), jnp.float32))
    return pl.pallas_call(
        functools.partial(exchange_kernel, kind, rim, modes, pix),
        out_shape=outs,
        in_specs=[VMEM] * len(operands),
        out_specs=tuple([VMEM] * len(outs)),
        scratch_shapes=scratch,
        compiler_params=pltpu.CompilerParams(
            collective_id=ident, has_side_effects=True, vmem_limit_bytes=LIMIT
        ),
        name="exchange_" + kind,
    )(*operands)


def on_device(object_field, probe, patterns, row_scales, positions, counts):
    modes, pix = probe.shape[1], probe.shape[2]
    rim = pix // 2
    tables = [jnp.asarray(t) for t in dft_tables(pix)]
    starts = positions[0, 0]
    step = math.lcm(8 * lax.axis_size("row") * lax.axis_size("col"), pix)
    rows_padded = -(-(2 * modes + 1) * pix // step) * step
    shape = (2, object_field.shape[1] + pix, object_field.shape[2] + pix)
    ext, amp = exchange("rim", 0, shape, pix, (object_field, patterns[0, 0], row_scales[0, 0]))
    for pass_number in range(PASSES):
        upd, sums = run_pass(ext, probe, amp, starts, counts, tables, rows_padded)
        kind = "tile" if pass_number == PASSES - 1 else "all"
        ext, probe = exchange(kind, pass_number + 1, shape, pix, (upd, ext, probe, sums))
    return (ext[:, rim:-rim, rim:-rim], probe)


def solution(mesh):
    placed = (
        P(None, "row", "col"),
        P(),
        P("row", "col", None, None, None),
        P("row", "col", None, None),
        P("row", "col", None, None),
        P("row", "col"),
    )
    return jax.shard_map(
        on_device,
        mesh=mesh,
        in_specs=placed,
        out_specs=(P(None, "row", "col"), P()),
        check_vma=False,
    )
```

```python
import functools
import math

import jax
import jax.numpy as jnp
import numpy as np
from jax import lax
from jax.experimental import pallas as pl
from jax.experimental.pallas import tpu as pltpu
from jax.sharding import PartitionSpec as P

PASSES = 2
TOGETHER = 2
MESH = pl.DeviceIdType.MESH
VMEM = pl.BlockSpec(memory_space=pltpu.VMEM)
HBM = pl.BlockSpec(memory_space=pltpu.HBM)
SMEM = pl.BlockSpec(memory_space=pltpu.SMEM)
LIMIT = 48 * 1024 * 1024


def dft_tables(length):
    index = np.arange(length)
    angle = (index[:, None] * index[None, :] % length) * (2.0 * math.pi / length)
    cosine, sine = np.cos(angle), np.sin(angle)
    forward = np.block([[cosine, -sine], [sine, cosine]]).astype(np.float32)
    inverse = np.block([[cosine, sine], [-sine, cosine]]).astype(np.float32)
    out = []
    for table in (forward, inverse):
        high = table.astype(jnp.bfloat16)
        out.append(np.stack([high, (table - high.astype(np.float32)).astype(jnp.bfloat16)]))
    return np.stack(out)


def split(value, axis):
    high = value.astype(jnp.bfloat16)
    low = (value - high.astype(jnp.float32)).astype(jnp.bfloat16)
    return jnp.concatenate([high, low, high], axis)


def times_table(value, table):
    high, low = table[0], table[1]
    joined = jnp.concatenate([high, high, low], 0)
    return jnp.dot(split(value, 1), joined, preferred_element_type=jnp.float32)


def table_times(table, value):
    high, low = table[0], table[1]
    joined = jnp.concatenate([high, high, low], 1)
    return jnp.dot(joined, split(value, 0), preferred_element_type=jnp.float32)


def pass_kernel(
    pos, count, ext, probe, amp, table, upd, sums, power, far, wave
):
    forward, inverse = table.at[0], table.at[1]
    modes, pix = probe.shape[1], probe.shape[2]
    group = 2 if modes % 2 == 0 else 1
    firsts = range(0, modes, group)
    together = wave.shape[0]
    last = pos.shape[0] - 1
    tall = pix + 8
    upd[...] = jnp.zeros_like(upd)
    sums[...] = jnp.zeros_like(sums)
    power[...] = jnp.sum(probe[0] * probe[0] + probe[1] * probe[1], axis=0)

    def body(step, carry):
        at = [jnp.minimum(step * together + k, last) for k in range(together)]
        places = []
        for k, p in enumerate(at):
            row, col = pos[p, 0], pos[p, 1]
            shift, down = lax.rem(col, pix), lax.rem(row, 8)
            rows = pl.ds(pl.multiple_of(row // 8 * 8, 8), tall)
            lanes = pl.ds(pl.multiple_of(col // pix * pix, pix), 2 * pix)
            places.append((rows, lanes, shift, down))
            live = jnp.where(step * together + k < count[0, 0], 1.0, 0.0).astype(jnp.float32)
            for plane in range(2):
                moved = pltpu.roll(ext[plane, rows, lanes], lax.rem(2 * pix - shift, 2 * pix), 1)
                moved = pltpu.roll(moved[:, :pix], lax.rem(tall - down, tall), 0)[:pix]
                wave[k, plane] = moved * live
        halves, intensity = {}, [None] * together
        for first in firsts:
            for k in range(together):
                o_re, o_im = wave[k, 0], wave[k, 1]
                exits = []
                for m in range(first, first + group):
                    p_re, p_im = probe[0, m], probe[1, m]
                    exits.append(
                        jnp.concatenate([p_re * o_re - p_im * o_im, p_re * o_im + p_im * o_re], 1)
                    )
                halves[k, first] = times_table(jnp.concatenate(exits, 0), forward)
        for first in firsts:
            for k in range(together):
                parts = [halves[k, first][j * pix : (j + 1) * pix] for j in range(group)]
                stacked = jnp.concatenate(
                    [jnp.concatenate([x[:, :pix], x[:, pix:]], 0) for x in parts], 1
                )
                full = table_times(inverse, stacked)
                far[k, :, first * pix : (first + group) * pix] = full
                for j in range(group):
                    block = full[:, j * pix : (j + 1) * pix]
                    term = block[:pix] * block[:pix] + block[pix:] * block[pix:]
                    intensity[k] = term if intensity[k] is None else intensity[k] + term
        factors = []
        for k, p in enumerate(at):
            size = jnp.maximum(jnp.sqrt(intensity[k]) * (1.0 / pix), 0.5)
            factors.append(amp[p] / size * (1.0 / (pix * pix)))
        for first in firsts:
            for k in range(together):
                both = jnp.concatenate([factors[k]] * 2, 0)
                scaled = far[k, :, first * pix : (first + group) * pix]
                scaled = scaled * jnp.concatenate([both] * group, 1)
                halves[k, first] = table_times(forward, scaled)
        change = [None] * together
        for first in firsts:
            grown = [None] * (2 * group)
            for k in range(together):
                o_re, o_im = wave[k, 0], wave[k, 1]
                parts = [halves[k, first][:, j * pix : (j + 1) * pix] for j in range(group)]
                flat = jnp.concatenate(
                    [jnp.concatenate([x[:pix], x[pix:]], 1) for x in parts], 0
                )
                back = times_table(flat, inverse)
                if change[k] is None:
                    change[k] = [-power[...] * o_re, -power[...] * o_im]
                for j in range(group):
                    b_re = back[j * pix : (j + 1) * pix, :pix]
                    b_im = back[j * pix : (j + 1) * pix, pix:]
                    p_re, p_im = probe[0, first + j], probe[1, first + j]
                    change[k][0] += p_re * b_re + p_im * b_im
                    change[k][1] += p_re * b_im - p_im * b_re
                    for part, term in (
                        (2 * j, o_re * b_re + o_im * b_im),
                        (2 * j + 1, o_re * b_im - o_im * b_re),
                    ):
                        grown[part] = term if grown[part] is None else grown[part] + term
            for j in range(group):
                sums[first + j] += grown[2 * j]
                sums[modes + first + j] += grown[2 * j + 1]
        sums[2 * modes] += sum(
            wave[k, 0] * wave[k, 0] + wave[k, 1] * wave[k, 1] for k in range(together)
        )
        for k, (rows, lanes, shift, down) in enumerate(places):
            for plane in range(2):
                moved = jnp.concatenate([change[k][plane], jnp.zeros((8, pix), jnp.float32)], 0)
                moved = pltpu.roll(moved, down, 0)
                moved = jnp.concatenate([moved, jnp.zeros_like(moved)], 1)
                upd[plane, rows, lanes] += pltpu.roll(moved, shift, 1)
        return carry

    lax.fori_loop(0, (count[0, 0] + together - 1) // together, body, 0)


def run_pass(ext, probe, amp, starts, counts, table, rows_padded):
    modes, pix = probe.shape[1], probe.shape[2]
    planes = rows_padded // pix
    return pl.pallas_call(
        pass_kernel,
        out_shape=(
            jax.ShapeDtypeStruct(ext.shape, jnp.float32),
            jax.ShapeDtypeStruct((planes, pix, pix), jnp.float32),
        ),
        in_specs=[SMEM, SMEM] + [VMEM] * 4,
        out_specs=(VMEM, VMEM),
        scratch_shapes=[
            pltpu.VMEM((pix, pix), jnp.float32),
            pltpu.VMEM((TOGETHER, 2 * pix, modes * pix), jnp.float32),
            pltpu.VMEM((TOGETHER, 2, pix, pix), jnp.float32),
        ],
        compiler_params=pltpu.CompilerParams(vmem_limit_bytes=LIMIT),
        name="scan_pass",
    )(starts, counts, ext, probe, amp, table)


def col_factors(n_row, n_col):
    core = math.gcd(2, n_col)
    far = math.gcd(4, n_col // core)
    return core, n_row * (n_col // core // far), far


def half_pack(re, im, upper):
    width = re.shape[-1]
    lane = lax.broadcasted_iota(jnp.int32, re.shape, 1)
    if upper:
        return jnp.where(lane < width // 2, pltpu.roll(re, width // 2, 1), im)
    return jnp.where(lane < width // 2, re, pltpu.roll(im, width // 2, 1))


def half_unpack(packed, upper):
    width = packed.shape[-1]
    lane = lax.broadcasted_iota(jnp.int32, packed.shape, 1)
    turned = pltpu.roll(packed, width // 2, 1)
    if upper:
        inside = lane >= width // 2
        return jnp.where(inside, turned, 0.0), jnp.where(inside, packed, 0.0)
    inside = lane < width // 2
    return jnp.where(inside, packed, 0.0), jnp.where(inside, turned, 0.0)


def partners(stage):
    size, mine, where = stage
    found = []
    for d in range(1, size):
        q = lax.rem(mine + d, size)
        row, col = where(q)
        found.append((q, {"row": row, "col": col}))
    return found


def exchange_kernel(kind, rim, modes, pix, *refs):
    reduce = kind != "rim"
    if reduce:
        (upd, ext, probe, sums, ext_out, probe_out) = refs[:6]
        scratch = refs[6:]
    else:
        (field_in, patterns_in, scales_in, table, probe, ext_out, amp, table_out, probe_out) = refs[:9]
        scratch = refs[9:]
        field, patterns, scales, local = scratch[11:]
        field_copy = pltpu.make_async_copy(field_in, field, local.at[0])
        pattern_copy = pltpu.make_async_copy(patterns_in, patterns, local.at[1])
        scale_copy = pltpu.make_async_copy(scales_in, scales, local.at[2])
        keep_table = pltpu.make_async_copy(table, table_out, local.at[3])
        keep_probe = pltpu.make_async_copy(probe, probe_out, local.at[4])
        field_copy.start()
        pattern_copy.start()
        scale_copy.start()
    work, low_r, high_r, low_c, high_c, low_s, high_s, send_r, recv_r, send_c, recv_c = scratch[:11]
    full_rows, full_cols = work.shape[1], work.shape[2]
    wide = 2 * rim
    packed = kind != "all"
    if kind == "rim":
        send_high, send_low = (full_rows - wide, rim), (rim, rim)
        put_low, put_high = (0, rim), (full_rows - rim, rim)
    elif kind == "all":
        send_high, send_low = (full_rows - wide, wide), (0, wide)
        put_low, put_high = (0, wide), (full_rows - wide, wide)
    else:
        send_high, send_low = (full_rows - rim, rim), (0, rim)
        put_low, put_high = (rim, rim), (full_rows - wide, rim)
    put_middle = (sum(put_low), put_high[0] - sum(put_low))
    top = put_low[0]
    blocks = [put_low, put_middle, put_high]
    n_row, n_col = lax.axis_size("row"), lax.axis_size("col")
    me_row, me_col = lax.axis_index("row"), lax.axis_index("col")
    row_low, row_high = me_row > 0, me_row < n_row - 1
    col_low, col_high = me_col > 0, me_col < n_col - 1

    barrier = pltpu.get_barrier_semaphore()

    def greet(target):
        pl.semaphore_signal(barrier, inc=1, device_id=target, device_id_type=MESH)

    pl.when(row_low)(lambda: greet({"row": me_row - 1}))
    pl.when(row_high)(lambda: greet({"row": me_row + 1}))
    pl.when(col_low)(lambda: greet({"col": me_col - 1}))
    pl.when(col_high)(lambda: greet({"col": me_col + 1}))
    greeted = sum(x.astype(jnp.int32) for x in (row_low, row_high, col_low, col_high))
    chunks = []
    if reduce:
        core, plane, far = col_factors(n_row, n_col)
        near = plane // n_row
        c = lax.rem(me_col, core)
        y = lax.rem(lax.div(me_col, core), near)
        z = lax.div(me_col, core * near)

        def in_core(q):
            return me_row, me_col + q - c

        def in_plane(q):
            return lax.div(q, near), me_col + (lax.rem(q, near) - y) * core

        def across(q):
            return me_row, me_col + (q - z) * (near * core)

        in_chip = (core, c, in_core)
        planar = (plane, me_row * near + y, in_plane)
        distant = (far, z, across)
        for order in ((in_chip, planar, distant), (in_chip, distant, planar)):
            chunks.append([stage for stage in order if stage[0] > 1])
        for stage in chunks[0]:
            for _, target in partners(stage):
                greet(target)
        greeted = greeted + sum(stage[0] - 1 for stage in chunks[0])

    if reduce:
        border = upd
    else:
        border = work
        blank = jnp.zeros((field.shape[1], wide), jnp.float32)
        work[...] = jnp.zeros_like(work)
        field_copy.wait()
        for k in range(2):
            work[k, rim:-rim, :] = pltpu.roll(jnp.concatenate([field[k], blank], 1), rim, 1)
    pl.semaphore_wait(barrier, greeted)

    def copy_to(src, dst, send, recv, target):
        return pltpu.make_async_remote_copy(
            src_ref=src,
            dst_ref=dst,
            send_sem=send,
            recv_sem=recv,
            device_id=target,
            device_id_type=MESH,
        )

    row_up = copy_to(
        border.at[:, pl.ds(*send_high), :], low_r, send_r.at[0], recv_r.at[0], {"row": me_row + 1}
    )
    row_down = copy_to(
        border.at[:, pl.ds(*send_low), :], high_r, send_r.at[1], recv_r.at[1], {"row": me_row - 1}
    )

    def start_rows():
        pl.when(row_high)(row_up.start)
        pl.when(row_low)(row_down.start)

    col_up, col_down = [], []
    for index, (start, length) in enumerate(blocks):
        at = pl.ds(start - top, length)
        if packed:
            sources = high_s.at[at, :], low_s.at[at, :]
            places = low_c.at[at, :], high_c.at[at, :]
        else:
            span = pl.ds(start, length)
            sources = work.at[:, span, pl.ds(full_cols - wide, wide)], work.at[:, span, pl.ds(0, wide)]
            places = low_c.at[:, at, :], high_c.at[:, at, :]
        sems = send_c.at[0, index], recv_c.at[0, index]
        col_up.append(copy_to(sources[0], places[0], *sems, {"col": me_col + 1}))
        sems = send_c.at[1, index], recv_c.at[1, index]
        col_down.append(copy_to(sources[1], places[1], *sems, {"col": me_col - 1}))

    def start_block(index):
        start, length = blocks[index]
        if packed:
            span, at = pl.ds(start, length), pl.ds(start - top, length)
            high, low = pl.ds(full_cols - wide, wide), pl.ds(0, wide)
            upper = kind == "tile"
            high_s[at, :] = half_pack(work[0, span, high], work[1, span, high], upper)
            low_s[at, :] = half_pack(work[0, span, low], work[1, span, low], not upper)
        pl.when(col_high)(col_up[index].start)
        pl.when(col_low)(col_down[index].start)

    def begin_cols():
        if reduce:
            work[...] = upd[...]
        start_block(1)
        pl.when(jnp.logical_not(row_low))(lambda: start_block(0))
        pl.when(jnp.logical_not(row_high))(lambda: start_block(2))

    def finish_rows():
        @pl.when(row_low)
        def _():
            row_up.wait_recv()
            work[:, pl.ds(*put_low), :] += low_r[...]
            start_block(0)

        @pl.when(row_high)
        def _():
            row_down.wait_recv()
            work[:, pl.ds(*put_high), :] += high_r[...]
            start_block(2)

    def finish_cols():
        ext_out[...] = work[...]
        span = pl.ds(top, sum(put_high) - top)

        def land(copies, buffer, start, upper):
            for copy in copies:
                copy.wait_recv()
            lanes = pl.ds(start, wide)
            if packed:
                re, im = half_unpack(buffer[...], upper)
                ext_out[0, span, lanes] += re
                ext_out[1, span, lanes] += im
            else:
                ext_out[:, span, lanes] += buffer[...]

        pl.when(col_low)(lambda: land(col_up, low_c, 0, kind == "tile"))
        pl.when(col_high)(lambda: land(col_down, high_c, full_cols - wide, kind != "tile"))

    def drain():
        pl.when(row_high)(row_up.wait_send)
        pl.when(row_low)(row_down.wait_send)
        for index in range(3):
            pl.when(col_high)(col_up[index].wait_send)
            pl.when(col_low)(col_down[index].wait_send)

    if not reduce:
        start_rows()
        begin_cols()
        keep_table.start()
        keep_probe.start()
        pattern_copy.wait()
        scale_copy.wait()
        for p in range(amp.shape[0]):
            column = jnp.broadcast_to(scales[p : p + 1, :], (pix, pix)).T
            amp[p] = patterns[p].astype(jnp.float32) * column
        finish_rows()
        finish_cols()
        keep_table.wait()
        keep_probe.wait()
        drain()
        return

    acc, gat, send_s, recv_s, send_g, recv_g = scratch[11:17]
    landings = scratch[17:]
    pending = []
    acc[...] = sums[...].reshape(acc.shape)
    half = acc.shape[0] // 2
    states = []
    for index, stages in enumerate(chunks):
        spans, offset, length, slot = [], index * half, half, 0
        for size, mine, _ in stages[:-1]:
            length //= size
            spans.append((offset, length, slot))
            offset, slot = offset + mine * length, slot + size - 1
        spans.append((offset, length, slot))
        states.append((stages, spans, landings[index * len(stages) : (index + 1) * len(stages)]))

    def rows_of(start, piece):
        return pl.ds(pl.multiple_of(start, 8), piece)

    def begin(index, step):
        stages, spans, lands = states[index]
        back = step >= len(stages)
        at = 2 * len(stages) - 2 - step if back else step
        stage = stages[at]
        size, mine, _ = stage
        start, piece, slot = spans[at]
        own = rows_of(start + mine * piece, piece)
        copies = []
        for d, (q, target) in enumerate(partners(stage)):
            sems = send_s.at[index, slot + d], recv_s.at[index, slot + d]
            if back:
                sems = send_g.at[index, slot + d], recv_g.at[index, slot + d]
                src, dst = gat.at[own], gat.at[own]
            elif at == len(stages) - 1:
                src, dst = acc.at[rows_of(start, piece)], lands[at].at[mine]
            else:
                src, dst = acc.at[rows_of(start + q * piece, piece)], lands[at].at[d]
            copies.append(copy_to(src, dst, *sems, target))
            copies[-1].start()
        pending.extend(copies)
        return copies

    def end(index, step, copies):
        stages, spans, lands = states[index]
        back = step >= len(stages)
        at = 2 * len(stages) - 2 - step if back else step
        stage = stages[at]
        size, mine, _ = stage
        start, piece, slot = spans[at]
        if not back and at < len(stages) - 1:
            keep = rows_of(start + mine * piece, piece)
            total = acc[keep, :]
            for d, copy in enumerate(copies):
                copy.wait_recv()
                total = total + lands[at][d]
            acc[keep, :] = total
            return
        if not back:
            lands[at][mine] = acc[rows_of(start, piece), :]
        for d, (_, target) in enumerate(partners(stage)):
            sender = lax.rem(mine + size - 1 - d, size)
            if back:
                place = gat.at[rows_of(start + sender * piece, piece)]
                sems = send_g.at[index, slot + d], recv_g.at[index, slot + d]
            else:
                place = lands[at].at[sender]
                sems = send_s.at[index, slot + d], recv_s.at[index, slot + d]
            copy_to(place, place, *sems, target).wait_recv()
        if not back:
            total = lands[at][0]
            for q in range(1, size):
                total = total + lands[at][q]
            gat[rows_of(start, piece), :] = total

    steps = 2 * len(chunks[0]) - 1
    flying = [None, None]
    for step in range(steps):
        for index in range(2):
            if step > 0:
                end(index, step - 1, flying[index])
            flying[index] = begin(index, step)
        if step == (0 if kind == "all" else min(1, steps - 1)):
            start_rows()
            begin_cols()
        if step == max(steps - 2, 0):
            finish_rows()
    finish_cols()
    peak = jnp.max(jnp.sum(probe[0] * probe[0] + probe[1] * probe[1], axis=0))
    change = ext_out[...] / peak
    if kind == "all":
        rows_at = lax.broadcasted_iota(jnp.int32, (full_rows, full_cols), 0)
        cols_at = lax.broadcasted_iota(jnp.int32, (full_rows, full_cols), 1)
        first_row = jnp.where(me_row == 0, rim, 0)
        last_row = jnp.where(me_row == n_row - 1, full_rows - rim, full_rows)
        first_col = jnp.where(me_col == 0, rim, 0)
        last_col = jnp.where(me_col == n_col - 1, full_cols - rim, full_cols)
        inside = (rows_at >= first_row) & (rows_at < last_row)
        inside = inside & (cols_at >= first_col) & (cols_at < last_col)
        change = jnp.where(inside[None], change, 0.0)
    ext_out[...] = ext[...] + change
    for index in range(2):
        end(index, steps - 1, flying[index])

    weight = gat[pl.ds(2 * modes * pix, pix), :]
    for k in range(2):
        for m in range(modes):
            probe_out[k, m] = gat[pl.ds((k * modes + m) * pix, pix), :] / weight
    for copy in pending:
        copy.wait_send()
    drain()


def exchange(kind, ident, shape, pix, operands):
    rim = pix // 2
    full_rows, full_cols = shape[1], shape[2]
    wide = 2 * rim
    row_width = wide if kind == "all" else rim
    height = full_rows - wide if kind == "tile" else full_rows
    n_row, n_col = lax.axis_size("row"), lax.axis_size("col")
    side = (2, height, wide) if kind == "all" else (height, wide)
    scratch = [
        pltpu.VMEM(shape, jnp.float32),
        pltpu.VMEM((2, row_width, full_cols), jnp.float32),
        pltpu.VMEM((2, row_width, full_cols), jnp.float32),
    ]
    scratch += [pltpu.VMEM(side, jnp.float32)] * 4
    scratch += [pltpu.SemaphoreType.DMA((2,))] * 2
    scratch += [pltpu.SemaphoreType.DMA((2, 3))] * 2
    out = jax.ShapeDtypeStruct(shape, jnp.float32)
    modes = 0
    if kind == "rim":
        field, patterns, scales, table, probe = operands
        outs = (
            out,
            jax.ShapeDtypeStruct(patterns.shape, jnp.float32),
            jax.ShapeDtypeStruct(table.shape, table.dtype),
            jax.ShapeDtypeStruct(probe.shape, jnp.float32),
        )
        scratch += [pltpu.VMEM(x.shape, x.dtype) for x in (field, patterns, scales)]
        scratch.append(pltpu.SemaphoreType.DMA((5,)))
    else:
        probe, sums = operands[2:]
        modes = probe.shape[1]
        outs = (out, jax.ShapeDtypeStruct(probe.shape, jnp.float32))
        rows = sums.shape[0] * pix
        core, plane, far = col_factors(n_row, n_col)
        hops = core + plane + far - 3
        scratch += [pltpu.VMEM((rows, pix), jnp.float32)] * 2
        scratch += [pltpu.SemaphoreType.DMA((2, hops))] * 4
        for order in ((core, plane, far), (core, far, plane)):
            sizes = [f for f in order if f > 1]
            length = rows // 2
            for size in sizes[:-1]:
                length //= size
                scratch.append(pltpu.VMEM((size - 1, length, pix), jnp.float32))
            scratch.append(pltpu.VMEM((sizes[-1], length, pix), jnp.float32))
    return pl.pallas_call(
        functools.partial(exchange_kernel, kind, rim, modes, pix),
        out_shape=outs,
        in_specs=[HBM if kind == "rim" else VMEM] * len(operands),
        out_specs=tuple([VMEM] * len(outs)),
        scratch_shapes=scratch,
        compiler_params=pltpu.CompilerParams(
            collective_id=ident, has_side_effects=True, vmem_limit_bytes=LIMIT
        ),
        name="exchange_" + kind,
    )(*operands)


def on_device(object_field, probe, patterns, row_scales, positions, counts):
    modes, pix = probe.shape[1], probe.shape[2]
    rim = pix // 2
    table = jnp.asarray(dft_tables(pix))
    starts = positions[0, 0]
    core, plane, far = col_factors(lax.axis_size("row"), lax.axis_size("col"))
    step = math.lcm(16 * core * max(plane, far), pix)
    rows_padded = -(-(2 * modes + 1) * pix // step) * step
    shape = (2, object_field.shape[1] + pix, object_field.shape[2] + pix)
    ext, amp, table, probe = exchange(
        "rim", 0, shape, pix, (object_field, patterns[0, 0], row_scales[0, 0], table, probe)
    )
    for pass_number in range(PASSES):
        upd, sums = run_pass(ext, probe, amp, starts, counts, table, rows_padded)
        kind = "tile" if pass_number == PASSES - 1 else "all"
        ext, probe = exchange(kind, pass_number + 1, shape, pix, (upd, ext, probe, sums))
    return (ext[:, rim:-rim, rim:-rim], probe)


def solution(mesh):
    placed = (
        P(None, "row", "col"),
        P(),
        P("row", "col", None, None, None),
        P("row", "col", None, None),
        P("row", "col", None, None),
        P("row", "col"),
    )
    return jax.shard_map(
        on_device,
        mesh=mesh,
        in_specs=placed,
        out_specs=(P(None, "row", "col"), P()),
        check_vma=False,
    )
```

```python
import functools
import math

import jax
import jax.numpy as jnp
from jax import lax
from jax.experimental import pallas as pl
from jax.experimental.pallas import tpu as pltpu
from jax.sharding import PartitionSpec as P

PASSES = 2
TOGETHER = 4
MESH = pl.DeviceIdType.MESH
VMEM = pl.BlockSpec(memory_space=pltpu.VMEM)
SMEM = pl.BlockSpec(memory_space=pltpu.SMEM)
LIMIT = 48 * 1024 * 1024


def write_tables(table, length):
    first = lax.broadcasted_iota(jnp.int32, (length, length), 0)
    second = lax.broadcasted_iota(jnp.int32, (length, length), 1)
    angle = lax.rem(first * second, length).astype(jnp.float32) * (2.0 * math.pi / length)
    parts = []
    for value in (jnp.cos(angle), jnp.sin(angle)):
        high = value.astype(jnp.bfloat16)
        parts.append((high, (value - high.astype(jnp.float32)).astype(jnp.bfloat16)))
    for k in range(2):
        cosine, sine = parts[0][k], parts[1][k]
        for index, (above, below) in enumerate(((-sine, sine), (sine, -sine))):
            table[index, k, :length, :length] = cosine
            table[index, k, :length, length:] = above
            table[index, k, length:, :length] = below
            table[index, k, length:, length:] = cosine


def split(value, axis):
    high = value.astype(jnp.bfloat16)
    low = (value - high.astype(jnp.float32)).astype(jnp.bfloat16)
    return jnp.concatenate([high, low, high], axis)


def times_table(value, table):
    high, low = table[0], table[1]
    joined = jnp.concatenate([high, high, low], 0)
    return jnp.dot(split(value, 1), joined, preferred_element_type=jnp.float32)


def table_times(table, value):
    high, low = table[0], table[1]
    joined = jnp.concatenate([high, high, low], 1)
    return jnp.dot(joined, split(value, 0), preferred_element_type=jnp.float32)


def pass_kernel(
    pos, count, ext, probe, amp, table, upd, sums, power, far, wave
):
    forward, inverse = table.at[0], table.at[1]
    modes, pix = probe.shape[1], probe.shape[2]
    group = 2 if modes % 2 == 0 else 1
    firsts = range(0, modes, group)
    together = wave.shape[0]
    last = pos.shape[1] - 1
    tall = pix + 8
    upd[...] = jnp.zeros_like(upd)
    sums[...] = jnp.zeros_like(sums)
    power[...] = jnp.sum(probe[0] * probe[0] + probe[1] * probe[1], axis=0)

    def body(step, carry):
        at = [jnp.minimum(step * together + k, last) for k in range(together)]
        places = []
        for k, p in enumerate(at):
            row, col = pos[0, p], pos[1, p]
            shift, down = lax.rem(col, pix), lax.rem(row, 8)
            rows = pl.ds(pl.multiple_of(row // 8 * 8, 8), tall)
            lanes = pl.ds(pl.multiple_of(col // pix * pix, pix), 2 * pix)
            places.append((rows, lanes, shift, down))
            live = jnp.where(step * together + k < count[0, 0], 1.0, 0.0).astype(jnp.float32)
            for plane in range(2):
                moved = pltpu.roll(ext[plane, rows, lanes], lax.rem(2 * pix - shift, 2 * pix), 1)
                moved = pltpu.roll(moved[:, :pix], lax.rem(tall - down, tall), 0)[:pix]
                wave[k, plane] = moved * live
        halves, intensity = {}, [None] * together
        for first in firsts:
            for k in range(together):
                o_re, o_im = wave[k, 0], wave[k, 1]
                exits = []
                for m in range(first, first + group):
                    p_re, p_im = probe[0, m], probe[1, m]
                    exits.append(
                        jnp.concatenate([p_re * o_re - p_im * o_im, p_re * o_im + p_im * o_re], 1)
                    )
                halves[k, first] = times_table(jnp.concatenate(exits, 0), forward)
        for first in firsts:
            for k in range(together):
                parts = [halves[k, first][j * pix : (j + 1) * pix] for j in range(group)]
                stacked = jnp.concatenate(
                    [jnp.concatenate([x[:, :pix], x[:, pix:]], 0) for x in parts], 1
                )
                full = table_times(inverse, stacked)
                far[k, :, first * pix : (first + group) * pix] = full
                for j in range(group):
                    block = full[:, j * pix : (j + 1) * pix]
                    term = block[:pix] * block[:pix] + block[pix:] * block[pix:]
                    intensity[k] = term if intensity[k] is None else intensity[k] + term
        factors = []
        for k, p in enumerate(at):
            size = jnp.maximum(jnp.sqrt(intensity[k]) * (1.0 / pix), 0.5)
            factors.append(amp[p] / size * (1.0 / (pix * pix)))
        for first in firsts:
            for k in range(together):
                both = jnp.concatenate([factors[k]] * 2, 0)
                scaled = far[k, :, first * pix : (first + group) * pix]
                scaled = scaled * jnp.concatenate([both] * group, 1)
                halves[k, first] = table_times(forward, scaled)
        change = [None] * together
        for first in firsts:
            grown = [None] * (2 * group)
            for k in range(together):
                o_re, o_im = wave[k, 0], wave[k, 1]
                parts = [halves[k, first][:, j * pix : (j + 1) * pix] for j in range(group)]
                flat = jnp.concatenate(
                    [jnp.concatenate([x[:pix], x[pix:]], 1) for x in parts], 0
                )
                back = times_table(flat, inverse)
                if change[k] is None:
                    change[k] = [-power[...] * o_re, -power[...] * o_im]
                for j in range(group):
                    b_re = back[j * pix : (j + 1) * pix, :pix]
                    b_im = back[j * pix : (j + 1) * pix, pix:]
                    p_re, p_im = probe[0, first + j], probe[1, first + j]
                    change[k][0] += p_re * b_re + p_im * b_im
                    change[k][1] += p_re * b_im - p_im * b_re
                    for part, term in (
                        (2 * j, o_re * b_re + o_im * b_im),
                        (2 * j + 1, o_re * b_im - o_im * b_re),
                    ):
                        grown[part] = term if grown[part] is None else grown[part] + term
            for j in range(group):
                sums[first + j] += grown[2 * j]
                sums[modes + first + j] += grown[2 * j + 1]
        sums[2 * modes] += sum(
            wave[k, 0] * wave[k, 0] + wave[k, 1] * wave[k, 1] for k in range(together)
        )
        for k, (rows, lanes, shift, down) in enumerate(places):
            for plane in range(2):
                moved = jnp.concatenate([change[k][plane], jnp.zeros((8, pix), jnp.float32)], 0)
                moved = pltpu.roll(moved, down, 0)
                moved = jnp.concatenate([moved, jnp.zeros_like(moved)], 1)
                upd[plane, rows, lanes] += pltpu.roll(moved, shift, 1)
        return carry

    lax.fori_loop(0, (count[0, 0] + together - 1) // together, body, 0)


def run_pass(ext, probe, amp, starts, counts, table, rows_padded):
    modes, pix = probe.shape[1], probe.shape[2]
    planes = rows_padded // pix
    return pl.pallas_call(
        pass_kernel,
        out_shape=(
            jax.ShapeDtypeStruct(ext.shape, jnp.float32),
            jax.ShapeDtypeStruct((planes, pix, pix), jnp.float32),
        ),
        in_specs=[SMEM, SMEM] + [VMEM] * 4,
        out_specs=(VMEM, VMEM),
        scratch_shapes=[
            pltpu.VMEM((pix, pix), jnp.float32),
            pltpu.VMEM((TOGETHER, 2 * pix, modes * pix), jnp.float32),
            pltpu.VMEM((TOGETHER, 2, pix, pix), jnp.float32),
        ],
        compiler_params=pltpu.CompilerParams(vmem_limit_bytes=LIMIT),
        name="scan_pass",
    )(starts, counts, ext, probe, amp, table)


def col_factors(n_row, n_col):
    core = math.gcd(2, n_col)
    far = math.gcd(4, n_col // core)
    return core, n_row * (n_col // core // far), far


def half_pack(re, im, upper):
    width = re.shape[-1]
    lane = lax.broadcasted_iota(jnp.int32, re.shape, 1)
    if upper:
        return jnp.where(lane < width // 2, pltpu.roll(re, width // 2, 1), im)
    return jnp.where(lane < width // 2, re, pltpu.roll(im, width // 2, 1))


def half_unpack(packed, upper):
    width = packed.shape[-1]
    lane = lax.broadcasted_iota(jnp.int32, packed.shape, 1)
    turned = pltpu.roll(packed, width // 2, 1)
    if upper:
        inside = lane >= width // 2
        return jnp.where(inside, turned, 0.0), jnp.where(inside, packed, 0.0)
    inside = lane < width // 2
    return jnp.where(inside, packed, 0.0), jnp.where(inside, turned, 0.0)


def partners(stage):
    size, mine, where = stage
    found = []
    for d in range(1, size):
        q = lax.rem(mine + d, size)
        row, col = where(q)
        found.append((q, {"row": row, "col": col}))
    return found


def exchange_kernel(kind, rim, modes, pix, *refs):
    reduce = kind != "rim"
    if reduce:
        (upd, ext, probe, sums, ext_out, probe_out) = refs[:6]
        scratch = refs[6:]
    else:
        (field, ext_out, table_out) = refs[:3]
        scratch = refs[3:]
    work, low_r, high_r, low_c, high_c, low_s, high_s, send_r, recv_r, send_c, recv_c = scratch[:11]
    full_rows, full_cols = work.shape[1], work.shape[2]
    wide = 2 * rim
    packed = kind != "all"
    if kind == "rim":
        send_high, send_low = (full_rows - wide, rim), (rim, rim)
        put_low, put_high = (0, rim), (full_rows - rim, rim)
    elif kind == "all":
        send_high, send_low = (full_rows - wide, wide), (0, wide)
        put_low, put_high = (0, wide), (full_rows - wide, wide)
    else:
        send_high, send_low = (full_rows - rim, rim), (0, rim)
        put_low, put_high = (rim, rim), (full_rows - wide, rim)
    put_middle = (sum(put_low), put_high[0] - sum(put_low))
    top = put_low[0]
    blocks = [put_low, put_middle, put_high]
    n_row, n_col = lax.axis_size("row"), lax.axis_size("col")
    me_row, me_col = lax.axis_index("row"), lax.axis_index("col")
    row_low, row_high = me_row > 0, me_row < n_row - 1
    col_low, col_high = me_col > 0, me_col < n_col - 1

    barrier = pltpu.get_barrier_semaphore()

    def greet(target):
        pl.semaphore_signal(barrier, inc=1, device_id=target, device_id_type=MESH)

    pl.when(row_low)(lambda: greet({"row": me_row - 1}))
    pl.when(row_high)(lambda: greet({"row": me_row + 1}))
    pl.when(col_low)(lambda: greet({"col": me_col - 1}))
    pl.when(col_high)(lambda: greet({"col": me_col + 1}))
    greeted = sum(x.astype(jnp.int32) for x in (row_low, row_high, col_low, col_high))
    chunks = []
    if reduce:
        core, plane, far = col_factors(n_row, n_col)
        near = plane // n_row
        c = lax.rem(me_col, core)
        y = lax.rem(lax.div(me_col, core), near)
        z = lax.div(me_col, core * near)

        def in_core(q):
            return me_row, me_col + q - c

        def in_plane(q):
            return lax.div(q, near), me_col + (lax.rem(q, near) - y) * core

        def across(q):
            return me_row, me_col + (q - z) * (near * core)

        in_chip = (core, c, in_core)
        planar = (plane, me_row * near + y, in_plane)
        distant = (far, z, across)
        for order in ((in_chip, planar, distant), (in_chip, distant, planar)):
            chunks.append([stage for stage in order if stage[0] > 1])
        for stage in chunks[0]:
            for _, target in partners(stage):
                greet(target)
        greeted = greeted + sum(stage[0] - 1 for stage in chunks[0])

    if reduce:
        border = upd
    else:
        border = work
        blank = jnp.zeros((field.shape[1], wide), jnp.float32)
        work[...] = jnp.zeros_like(work)
        for k in range(2):
            work[k, rim:-rim, :] = pltpu.roll(jnp.concatenate([field[k], blank], 1), rim, 1)
    pl.semaphore_wait(barrier, greeted)

    def copy_to(src, dst, send, recv, target):
        return pltpu.make_async_remote_copy(
            src_ref=src,
            dst_ref=dst,
            send_sem=send,
            recv_sem=recv,
            device_id=target,
            device_id_type=MESH,
        )

    row_up = copy_to(
        border.at[:, pl.ds(*send_high), :], low_r, send_r.at[0], recv_r.at[0], {"row": me_row + 1}
    )
    row_down = copy_to(
        border.at[:, pl.ds(*send_low), :], high_r, send_r.at[1], recv_r.at[1], {"row": me_row - 1}
    )

    def start_rows():
        pl.when(row_high)(row_up.start)
        pl.when(row_low)(row_down.start)

    col_up, col_down = [], []
    for index, (start, length) in enumerate(blocks):
        at = pl.ds(start - top, length)
        if packed:
            sources = high_s.at[at, :], low_s.at[at, :]
            places = low_c.at[at, :], high_c.at[at, :]
        else:
            span = pl.ds(start, length)
            sources = work.at[:, span, pl.ds(full_cols - wide, wide)], work.at[:, span, pl.ds(0, wide)]
            places = low_c.at[:, at, :], high_c.at[:, at, :]
        sems = send_c.at[0, index], recv_c.at[0, index]
        col_up.append(copy_to(sources[0], places[0], *sems, {"col": me_col + 1}))
        sems = send_c.at[1, index], recv_c.at[1, index]
        col_down.append(copy_to(sources[1], places[1], *sems, {"col": me_col - 1}))

    def start_block(index):
        start, length = blocks[index]
        if packed:
            span, at = pl.ds(start, length), pl.ds(start - top, length)
            high, low = pl.ds(full_cols - wide, wide), pl.ds(0, wide)
            upper = kind == "tile"
            high_s[at, :] = half_pack(work[0, span, high], work[1, span, high], upper)
            low_s[at, :] = half_pack(work[0, span, low], work[1, span, low], not upper)
        pl.when(col_high)(col_up[index].start)
        pl.when(col_low)(col_down[index].start)

    def begin_cols():
        if reduce:
            work[...] = upd[...]
        start_block(1)
        pl.when(jnp.logical_not(row_low))(lambda: start_block(0))
        pl.when(jnp.logical_not(row_high))(lambda: start_block(2))

    def finish_rows():
        @pl.when(row_low)
        def _():
            row_up.wait_recv()
            work[:, pl.ds(*put_low), :] += low_r[...]
            start_block(0)

        @pl.when(row_high)
        def _():
            row_down.wait_recv()
            work[:, pl.ds(*put_high), :] += high_r[...]
            start_block(2)

    def finish_cols():
        ext_out[...] = work[...]
        span = pl.ds(top, sum(put_high) - top)

        def land(copies, buffer, start, upper):
            for copy in copies:
                copy.wait_recv()
            lanes = pl.ds(start, wide)
            if packed:
                re, im = half_unpack(buffer[...], upper)
                ext_out[0, span, lanes] += re
                ext_out[1, span, lanes] += im
            else:
                ext_out[:, span, lanes] += buffer[...]

        pl.when(col_low)(lambda: land(col_up, low_c, 0, kind == "tile"))
        pl.when(col_high)(lambda: land(col_down, high_c, full_cols - wide, kind != "tile"))

    def drain():
        pl.when(row_high)(row_up.wait_send)
        pl.when(row_low)(row_down.wait_send)
        for index in range(3):
            pl.when(col_high)(col_up[index].wait_send)
            pl.when(col_low)(col_down[index].wait_send)

    if not reduce:
        start_rows()
        begin_cols()
        write_tables(table_out, pix)
        finish_rows()
        finish_cols()
        drain()
        return

    acc, gat, send_s, recv_s, send_g, recv_g = scratch[11:17]
    landings = scratch[17:]
    pending = []
    acc[...] = sums[...].reshape(acc.shape)
    half = acc.shape[0] // 2
    states = []
    for index, stages in enumerate(chunks):
        spans, offset, length, slot = [], index * half, half, 0
        for size, mine, _ in stages[:-1]:
            length //= size
            spans.append((offset, length, slot))
            offset, slot = offset + mine * length, slot + size - 1
        spans.append((offset, length, slot))
        states.append((stages, spans, landings[index * len(stages) : (index + 1) * len(stages)]))

    def rows_of(start, piece):
        return pl.ds(pl.multiple_of(start, 8), piece)

    def begin(index, step):
        stages, spans, lands = states[index]
        back = step >= len(stages)
        at = 2 * len(stages) - 2 - step if back else step
        stage = stages[at]
        size, mine, _ = stage
        start, piece, slot = spans[at]
        own = rows_of(start + mine * piece, piece)
        copies = []
        for d, (q, target) in enumerate(partners(stage)):
            sems = send_s.at[index, slot + d], recv_s.at[index, slot + d]
            if back:
                sems = send_g.at[index, slot + d], recv_g.at[index, slot + d]
                src, dst = gat.at[own], gat.at[own]
            elif at == len(stages) - 1:
                src, dst = acc.at[rows_of(start, piece)], lands[at].at[mine]
            else:
                src, dst = acc.at[rows_of(start + q * piece, piece)], lands[at].at[d]
            copies.append(copy_to(src, dst, *sems, target))
            copies[-1].start()
        pending.extend(copies)
        return copies

    def end(index, step, copies):
        stages, spans, lands = states[index]
        back = step >= len(stages)
        at = 2 * len(stages) - 2 - step if back else step
        stage = stages[at]
        size, mine, _ = stage
        start, piece, slot = spans[at]
        if not back and at < len(stages) - 1:
            keep = rows_of(start + mine * piece, piece)
            total = acc[keep, :]
            for d, copy in enumerate(copies):
                copy.wait_recv()
                total = total + lands[at][d]
            acc[keep, :] = total
            return
        if not back:
            lands[at][mine] = acc[rows_of(start, piece), :]
        for d, (_, target) in enumerate(partners(stage)):
            sender = lax.rem(mine + size - 1 - d, size)
            if back:
                place = gat.at[rows_of(start + sender * piece, piece)]
                sems = send_g.at[index, slot + d], recv_g.at[index, slot + d]
            else:
                place = lands[at].at[sender]
                sems = send_s.at[index, slot + d], recv_s.at[index, slot + d]
            copy_to(place, place, *sems, target).wait_recv()
        if not back:
            total = lands[at][0]
            for q in range(1, size):
                total = total + lands[at][q]
            gat[rows_of(start, piece), :] = total

    steps = 2 * len(chunks[0]) - 1
    flying = [None, None]
    for step in range(steps):
        for index in range(2):
            if step > 0:
                end(index, step - 1, flying[index])
            flying[index] = begin(index, step)
        if step == (0 if kind == "all" else min(1, steps - 1)):
            start_rows()
            begin_cols()
        if step == max(steps - 2, 0):
            finish_rows()
    finish_cols()
    peak = jnp.max(jnp.sum(probe[0] * probe[0] + probe[1] * probe[1], axis=0))
    change = ext_out[...] / peak
    if kind == "all":
        rows_at = lax.broadcasted_iota(jnp.int32, (full_rows, full_cols), 0)
        cols_at = lax.broadcasted_iota(jnp.int32, (full_rows, full_cols), 1)
        first_row = jnp.where(me_row == 0, rim, 0)
        last_row = jnp.where(me_row == n_row - 1, full_rows - rim, full_rows)
        first_col = jnp.where(me_col == 0, rim, 0)
        last_col = jnp.where(me_col == n_col - 1, full_cols - rim, full_cols)
        inside = (rows_at >= first_row) & (rows_at < last_row)
        inside = inside & (cols_at >= first_col) & (cols_at < last_col)
        change = jnp.where(inside[None], change, 0.0)
    ext_out[...] = ext[...] + change
    for index in range(2):
        end(index, steps - 1, flying[index])

    weight = gat[pl.ds(2 * modes * pix, pix), :]
    for k in range(2):
        for m in range(modes):
            probe_out[k, m] = gat[pl.ds((k * modes + m) * pix, pix), :] / weight
    for copy in pending:
        copy.wait_send()
    drain()


def exchange(kind, ident, shape, pix, operands):
    rim = pix // 2
    full_rows, full_cols = shape[1], shape[2]
    wide = 2 * rim
    row_width = wide if kind == "all" else rim
    height = full_rows - wide if kind == "tile" else full_rows
    n_row, n_col = lax.axis_size("row"), lax.axis_size("col")
    side = (2, height, wide) if kind == "all" else (height, wide)
    scratch = [
        pltpu.VMEM(shape, jnp.float32),
        pltpu.VMEM((2, row_width, full_cols), jnp.float32),
        pltpu.VMEM((2, row_width, full_cols), jnp.float32),
    ]
    scratch += [pltpu.VMEM(side, jnp.float32)] * 4
    scratch += [pltpu.SemaphoreType.DMA((2,))] * 2
    scratch += [pltpu.SemaphoreType.DMA((2, 3))] * 2
    out = jax.ShapeDtypeStruct(shape, jnp.float32)
    modes = 0
    if kind == "rim":
        outs = (out, jax.ShapeDtypeStruct((2, 2, 2 * pix, 2 * pix), jnp.bfloat16))
    else:
        probe, sums = operands[2:]
        modes = probe.shape[1]
        outs = (out, jax.ShapeDtypeStruct(probe.shape, jnp.float32))
        rows = sums.shape[0] * pix
        core, plane, far = col_factors(n_row, n_col)
        hops = core + plane + far - 3
        scratch += [pltpu.VMEM((rows, pix), jnp.float32)] * 2
        scratch += [pltpu.SemaphoreType.DMA((2, hops))] * 4
        for order in ((core, plane, far), (core, far, plane)):
            sizes = [f for f in order if f > 1]
            length = rows // 2
            for size in sizes[:-1]:
                length //= size
                scratch.append(pltpu.VMEM((size - 1, length, pix), jnp.float32))
            scratch.append(pltpu.VMEM((sizes[-1], length, pix), jnp.float32))
    return pl.pallas_call(
        functools.partial(exchange_kernel, kind, rim, modes, pix),
        out_shape=outs,
        in_specs=[VMEM] * len(operands),
        out_specs=tuple([VMEM] * len(outs)),
        scratch_shapes=scratch,
        compiler_params=pltpu.CompilerParams(
            collective_id=ident, has_side_effects=True, vmem_limit_bytes=LIMIT
        ),
        name="exchange_" + kind,
    )(*operands)


def on_device(object_field, probe, patterns, row_scales, positions, counts):
    modes, pix = probe.shape[1], probe.shape[2]
    rim = pix // 2
    starts = positions[0, 0].T
    amp = patterns[0, 0].astype(jnp.float32) * row_scales[0, 0][..., None]
    core, plane, far = col_factors(lax.axis_size("row"), lax.axis_size("col"))
    step = math.lcm(16 * core * max(plane, far), pix)
    rows_padded = -(-(2 * modes + 1) * pix // step) * step
    shape = (2, object_field.shape[1] + pix, object_field.shape[2] + pix)
    ext, table = exchange("rim", 0, shape, pix, (object_field,))
    for pass_number in range(PASSES):
        upd, sums = run_pass(ext, probe, amp, starts, counts, table, rows_padded)
        kind = "tile" if pass_number == PASSES - 1 else "all"
        ext, probe = exchange(kind, pass_number + 1, shape, pix, (upd, ext, probe, sums))
    return (ext[:, rim:-rim, rim:-rim], probe)


def solution(mesh):
    placed = (
        P(None, "row", "col"),
        P(),
        P("row", "col", None, None, None),
        P("row", "col", None, None),
        P("row", "col", None, None),
        P("row", "col"),
    )
    return jax.shard_map(
        on_device,
        mesh=mesh,
        in_specs=placed,
        out_specs=(P(None, "row", "col"), P()),
        check_vma=False,
    )
```

```python
import functools
import math

import jax
import jax.numpy as jnp
from jax import lax
from jax.experimental import pallas as pl
from jax.experimental.pallas import tpu as pltpu
from jax.sharding import PartitionSpec as P

PASSES = 2
TOGETHER = 4
MESH = pl.DeviceIdType.MESH
VMEM = pl.BlockSpec(memory_space=pltpu.VMEM)
SMEM = pl.BlockSpec(memory_space=pltpu.SMEM)
LIMIT = 48 * 1024 * 1024


def write_tables(table, length):
    first = lax.broadcasted_iota(jnp.int32, (length, length), 0)
    second = lax.broadcasted_iota(jnp.int32, (length, length), 1)
    angle = lax.rem(first * second, length).astype(jnp.float32) * (2.0 * math.pi / length)
    parts = []
    for value in (jnp.cos(angle), jnp.sin(angle)):
        high = value.astype(jnp.bfloat16)
        parts.append((high, (value - high.astype(jnp.float32)).astype(jnp.bfloat16)))
    for k in range(2):
        cosine, sine = parts[0][k], parts[1][k]
        for index, (above, below) in enumerate(((-sine, sine), (sine, -sine))):
            table[index, k, :length, :length] = cosine
            table[index, k, :length, length:] = above
            table[index, k, length:, :length] = below
            table[index, k, length:, length:] = cosine


def split(value, axis):
    high = value.astype(jnp.bfloat16)
    low = (value - high.astype(jnp.float32)).astype(jnp.bfloat16)
    return jnp.concatenate([high, low, high], axis)


def times_table(value, table):
    high, low = table[0], table[1]
    joined = jnp.concatenate([high, high, low], 0)
    return jnp.dot(split(value, 1), joined, preferred_element_type=jnp.float32)


def table_times(table, value):
    high, low = table[0], table[1]
    joined = jnp.concatenate([high, high, low], 1)
    return jnp.dot(joined, split(value, 0), preferred_element_type=jnp.float32)


def pass_kernel(
    pos, count, ext, probe, amp, table, upd, sums, power, far, wave
):
    forward, inverse = table.at[0], table.at[1]
    modes, pix = probe.shape[1], probe.shape[2]
    group = 2 if modes % 2 == 0 else 1
    firsts = range(0, modes, group)
    together = wave.shape[0]
    last = pos.shape[1] - 1
    tall = pix + 8
    upd[...] = jnp.zeros_like(upd)
    sums[...] = jnp.zeros_like(sums)
    power[...] = jnp.sum(probe[0] * probe[0] + probe[1] * probe[1], axis=0)

    def body(step, carry):
        at = [jnp.minimum(step * together + k, last) for k in range(together)]
        places = []
        for k, p in enumerate(at):
            row, col = pos[0, p], pos[1, p]
            shift, down = lax.rem(col, pix), lax.rem(row, 8)
            rows = pl.ds(pl.multiple_of(row // 8 * 8, 8), tall)
            lanes = pl.ds(pl.multiple_of(col // pix * pix, pix), 2 * pix)
            places.append((rows, lanes, shift, down))
            live = jnp.where(step * together + k < count[0, 0], 1.0, 0.0).astype(jnp.float32)
            for plane in range(2):
                moved = pltpu.roll(ext[plane, rows, lanes], lax.rem(2 * pix - shift, 2 * pix), 1)
                moved = pltpu.roll(moved[:, :pix], lax.rem(tall - down, tall), 0)[:pix]
                wave[k, plane] = moved * live
        halves, intensity = {}, [None] * together
        for first in firsts:
            for k in range(together):
                o_re, o_im = wave[k, 0], wave[k, 1]
                exits = []
                for m in range(first, first + group):
                    p_re, p_im = probe[0, m], probe[1, m]
                    exits.append(
                        jnp.concatenate([p_re * o_re - p_im * o_im, p_re * o_im + p_im * o_re], 1)
                    )
                halves[k, first] = times_table(jnp.concatenate(exits, 0), forward)
        for first in firsts:
            for k in range(together):
                parts = [halves[k, first][j * pix : (j + 1) * pix] for j in range(group)]
                stacked = jnp.concatenate(
                    [jnp.concatenate([x[:, :pix], x[:, pix:]], 0) for x in parts], 1
                )
                full = table_times(inverse, stacked)
                far[k, :, first * pix : (first + group) * pix] = full
                for j in range(group):
                    block = full[:, j * pix : (j + 1) * pix]
                    term = block[:pix] * block[:pix] + block[pix:] * block[pix:]
                    intensity[k] = term if intensity[k] is None else intensity[k] + term
        factors = []
        for k, p in enumerate(at):
            size = jnp.maximum(jnp.sqrt(intensity[k]) * (1.0 / pix), 0.5)
            factors.append(amp[p] / size * (1.0 / (pix * pix)))
        for first in firsts:
            for k in range(together):
                both = jnp.concatenate([factors[k]] * 2, 0)
                scaled = far[k, :, first * pix : (first + group) * pix]
                scaled = scaled * jnp.concatenate([both] * group, 1)
                halves[k, first] = table_times(forward, scaled)
        change = [None] * together
        for first in firsts:
            grown = [None] * (2 * group)
            for k in range(together):
                o_re, o_im = wave[k, 0], wave[k, 1]
                parts = [halves[k, first][:, j * pix : (j + 1) * pix] for j in range(group)]
                flat = jnp.concatenate(
                    [jnp.concatenate([x[:pix], x[pix:]], 1) for x in parts], 0
                )
                back = times_table(flat, inverse)
                if change[k] is None:
                    change[k] = [-power[...] * o_re, -power[...] * o_im]
                for j in range(group):
                    b_re = back[j * pix : (j + 1) * pix, :pix]
                    b_im = back[j * pix : (j + 1) * pix, pix:]
                    p_re, p_im = probe[0, first + j], probe[1, first + j]
                    change[k][0] += p_re * b_re + p_im * b_im
                    change[k][1] += p_re * b_im - p_im * b_re
                    for part, term in (
                        (2 * j, o_re * b_re + o_im * b_im),
                        (2 * j + 1, o_re * b_im - o_im * b_re),
                    ):
                        grown[part] = term if grown[part] is None else grown[part] + term
            for j in range(group):
                sums[first + j] += grown[2 * j]
                sums[modes + first + j] += grown[2 * j + 1]
        sums[2 * modes] += sum(
            wave[k, 0] * wave[k, 0] + wave[k, 1] * wave[k, 1] for k in range(together)
        )
        for k, (rows, lanes, shift, down) in enumerate(places):
            for plane in range(2):
                moved = jnp.concatenate([change[k][plane], jnp.zeros((8, pix), jnp.float32)], 0)
                moved = pltpu.roll(moved, down, 0)
                moved = jnp.concatenate([moved, jnp.zeros_like(moved)], 1)
                upd[plane, rows, lanes] += pltpu.roll(moved, shift, 1)
        return carry

    lax.fori_loop(0, (count[0, 0] + together - 1) // together, body, 0)


def run_pass(ext, probe, amp, starts, counts, table, rows_padded):
    modes, pix = probe.shape[1], probe.shape[2]
    planes = rows_padded // pix
    return pl.pallas_call(
        pass_kernel,
        out_shape=(
            jax.ShapeDtypeStruct(ext.shape, jnp.float32),
            jax.ShapeDtypeStruct((planes, pix, pix), jnp.float32),
        ),
        in_specs=[SMEM, SMEM] + [VMEM] * 4,
        out_specs=(VMEM, VMEM),
        scratch_shapes=[
            pltpu.VMEM((pix, pix), jnp.float32),
            pltpu.VMEM((TOGETHER, 2 * pix, modes * pix), jnp.float32),
            pltpu.VMEM((TOGETHER, 2, pix, pix), jnp.float32),
        ],
        compiler_params=pltpu.CompilerParams(vmem_limit_bytes=LIMIT),
        name="scan_pass",
    )(starts, counts, ext, probe, amp, table)


def col_factors(n_row, n_col):
    core = math.gcd(2, n_col)
    far = math.gcd(4, n_col // core)
    return core, n_row * (n_col // core // far), far


def half_pack(re, im, upper):
    width = re.shape[-1]
    lane = lax.broadcasted_iota(jnp.int32, re.shape, 1)
    if upper:
        return jnp.where(lane < width // 2, pltpu.roll(re, width // 2, 1), im)
    return jnp.where(lane < width // 2, re, pltpu.roll(im, width // 2, 1))


def half_unpack(packed, upper):
    width = packed.shape[-1]
    lane = lax.broadcasted_iota(jnp.int32, packed.shape, 1)
    turned = pltpu.roll(packed, width // 2, 1)
    if upper:
        inside = lane >= width // 2
        return jnp.where(inside, turned, 0.0), jnp.where(inside, packed, 0.0)
    inside = lane < width // 2
    return jnp.where(inside, packed, 0.0), jnp.where(inside, turned, 0.0)


def partners(stage):
    size, mine, where = stage
    found = []
    for d in range(1, size):
        q = lax.rem(mine + d, size)
        row, col = where(q)
        found.append((q, {"row": row, "col": col}))
    return found


def exchange_kernel(kind, rim, modes, pix, *refs):
    reduce = kind != "rim"
    if reduce:
        (upd, ext, probe, sums, ext_out, probe_out) = refs[:6]
        scratch = refs[6:]
    else:
        (field, ext_out, table_out) = refs[:3]
        scratch = refs[3:]
    work, low_r, high_r, low_c, high_c, low_s, high_s, send_r, recv_r, send_c, recv_c = scratch[:11]
    full_rows, full_cols = work.shape[1], work.shape[2]
    wide = 2 * rim
    packed = kind != "all"
    if kind == "rim":
        send_high, send_low = (full_rows - wide, rim), (rim, rim)
        put_low, put_high = (0, rim), (full_rows - rim, rim)
    elif kind == "all":
        send_high, send_low = (full_rows - wide, wide), (0, wide)
        put_low, put_high = (0, wide), (full_rows - wide, wide)
    else:
        send_high, send_low = (full_rows - rim, rim), (0, rim)
        put_low, put_high = (rim, rim), (full_rows - wide, rim)
    put_middle = (sum(put_low), put_high[0] - sum(put_low))
    top = put_low[0]
    blocks = [put_low, put_middle, put_high]
    n_row, n_col = lax.axis_size("row"), lax.axis_size("col")
    me_row, me_col = lax.axis_index("row"), lax.axis_index("col")
    row_low, row_high = me_row > 0, me_row < n_row - 1
    col_low, col_high = me_col > 0, me_col < n_col - 1

    barrier = pltpu.get_barrier_semaphore()

    def greet(target):
        pl.semaphore_signal(barrier, inc=1, device_id=target, device_id_type=MESH)

    pl.when(row_low)(lambda: greet({"row": me_row - 1}))
    pl.when(row_high)(lambda: greet({"row": me_row + 1}))
    pl.when(col_low)(lambda: greet({"col": me_col - 1}))
    pl.when(col_high)(lambda: greet({"col": me_col + 1}))
    greeted = sum(x.astype(jnp.int32) for x in (row_low, row_high, col_low, col_high))
    chunks = []
    if reduce:
        core, plane, far = col_factors(n_row, n_col)
        near = plane // n_row
        c = lax.rem(me_col, core)
        y = lax.rem(lax.div(me_col, core), near)
        z = lax.div(me_col, core * near)

        def in_core(q):
            return me_row, me_col + q - c

        def in_plane(q):
            return lax.div(q, near), me_col + (lax.rem(q, near) - y) * core

        def across(q):
            return me_row, me_col + (q - z) * (near * core)

        in_chip = (core, c, in_core)
        planar = (plane, me_row * near + y, in_plane)
        distant = (far, z, across)
        for order in ((in_chip, planar, distant), (in_chip, distant, planar)):
            chunks.append([stage for stage in order if stage[0] > 1])
        for stage in chunks[0]:
            for _, target in partners(stage):
                greet(target)
        greeted = greeted + sum(stage[0] - 1 for stage in chunks[0])

    if reduce:
        border = upd
    else:
        border = work
        blank = jnp.zeros((field.shape[1], wide), jnp.float32)
        work[...] = jnp.zeros_like(work)
        for k in range(2):
            work[k, rim:-rim, :] = pltpu.roll(jnp.concatenate([field[k], blank], 1), rim, 1)
    pl.semaphore_wait(barrier, greeted)

    def copy_to(src, dst, send, recv, target):
        return pltpu.make_async_remote_copy(
            src_ref=src,
            dst_ref=dst,
            send_sem=send,
            recv_sem=recv,
            device_id=target,
            device_id_type=MESH,
        )

    spans_r = [pl.ds(0, wide), pl.ds(full_cols - wide, wide), pl.ds(wide, full_cols - 2 * wide)]
    row_up, row_down = [], []
    for j, lanes in enumerate(spans_r):
        row_up.append(
            copy_to(
                border.at[:, pl.ds(*send_high), lanes],
                low_r.at[:, :, lanes],
                send_r.at[0, j],
                recv_r.at[0, j],
                {"row": me_row + 1},
            )
        )
        row_down.append(
            copy_to(
                border.at[:, pl.ds(*send_low), lanes],
                high_r.at[:, :, lanes],
                send_r.at[1, j],
                recv_r.at[1, j],
                {"row": me_row - 1},
            )
        )

    def start_rows():
        for j in range(3):
            pl.when(row_high)(row_up[j].start)
            pl.when(row_low)(row_down[j].start)

    def add_rows(copies, buffer, put, which):
        for j in which:
            copies[j].wait_recv()
            work[:, pl.ds(*put), spans_r[j]] += buffer[:, :, spans_r[j]]

    col_up, col_down = [], []
    for index, (start, length) in enumerate(blocks):
        at = pl.ds(start - top, length)
        if packed:
            sources = high_s.at[at, :], low_s.at[at, :]
            places = low_c.at[at, :], high_c.at[at, :]
        else:
            span = pl.ds(start, length)
            sources = work.at[:, span, pl.ds(full_cols - wide, wide)], work.at[:, span, pl.ds(0, wide)]
            places = low_c.at[:, at, :], high_c.at[:, at, :]
        sems = send_c.at[0, index], recv_c.at[0, index]
        col_up.append(copy_to(sources[0], places[0], *sems, {"col": me_col + 1}))
        sems = send_c.at[1, index], recv_c.at[1, index]
        col_down.append(copy_to(sources[1], places[1], *sems, {"col": me_col - 1}))

    def start_block(index):
        start, length = blocks[index]
        if packed:
            span, at = pl.ds(start, length), pl.ds(start - top, length)
            high, low = pl.ds(full_cols - wide, wide), pl.ds(0, wide)
            upper = kind == "tile"
            high_s[at, :] = half_pack(work[0, span, high], work[1, span, high], upper)
            low_s[at, :] = half_pack(work[0, span, low], work[1, span, low], not upper)
        pl.when(col_high)(col_up[index].start)
        pl.when(col_low)(col_down[index].start)

    def begin_cols():
        if reduce:
            work[...] = upd[...]
        start_block(1)
        pl.when(jnp.logical_not(row_low))(lambda: start_block(0))
        pl.when(jnp.logical_not(row_high))(lambda: start_block(2))

    def finish_rows():
        @pl.when(row_low)
        def _():
            add_rows(row_up, low_r, put_low, (0, 1))
            start_block(0)

        @pl.when(row_high)
        def _():
            add_rows(row_down, high_r, put_high, (0, 1))
            start_block(2)

    def finish_cols():
        pl.when(row_low)(lambda: add_rows(row_up, low_r, put_low, (2,)))
        pl.when(row_high)(lambda: add_rows(row_down, high_r, put_high, (2,)))
        ext_out[...] = work[...]
        span = pl.ds(top, sum(put_high) - top)

        def land(copies, buffer, start, upper):
            for copy in copies:
                copy.wait_recv()
            lanes = pl.ds(start, wide)
            if packed:
                re, im = half_unpack(buffer[...], upper)
                ext_out[0, span, lanes] += re
                ext_out[1, span, lanes] += im
            else:
                ext_out[:, span, lanes] += buffer[...]

        pl.when(col_low)(lambda: land(col_up, low_c, 0, kind == "tile"))
        pl.when(col_high)(lambda: land(col_down, high_c, full_cols - wide, kind != "tile"))

    def drain():
        for index in range(3):
            pl.when(row_high)(row_up[index].wait_send)
            pl.when(row_low)(row_down[index].wait_send)
            pl.when(col_high)(col_up[index].wait_send)
            pl.when(col_low)(col_down[index].wait_send)

    if not reduce:
        start_rows()
        begin_cols()
        write_tables(table_out, pix)
        finish_rows()
        finish_cols()
        drain()
        return

    acc, gat, send_s, recv_s, send_g, recv_g = scratch[11:17]
    landings = scratch[17:]
    pending = []
    acc[...] = sums[...].reshape(acc.shape)
    half = acc.shape[0] // 2
    states = []
    for index, stages in enumerate(chunks):
        spans, offset, length, slot = [], index * half, half, 0
        for size, mine, _ in stages[:-1]:
            length //= size
            spans.append((offset, length, slot))
            offset, slot = offset + mine * length, slot + size - 1
        spans.append((offset, length, slot))
        states.append((stages, spans, landings[index * len(stages) : (index + 1) * len(stages)]))

    def rows_of(start, piece):
        return pl.ds(pl.multiple_of(start, 8), piece)

    def begin(index, step):
        stages, spans, lands = states[index]
        back = step >= len(stages)
        at = 2 * len(stages) - 2 - step if back else step
        stage = stages[at]
        size, mine, _ = stage
        start, piece, slot = spans[at]
        own = rows_of(start + mine * piece, piece)
        copies = []
        for d, (q, target) in enumerate(partners(stage)):
            sems = send_s.at[index, slot + d], recv_s.at[index, slot + d]
            if back:
                sems = send_g.at[index, slot + d], recv_g.at[index, slot + d]
                src, dst = gat.at[own], gat.at[own]
            elif at == len(stages) - 1:
                src, dst = acc.at[rows_of(start, piece)], lands[at].at[mine]
            else:
                src, dst = acc.at[rows_of(start + q * piece, piece)], lands[at].at[d]
            copies.append(copy_to(src, dst, *sems, target))
            copies[-1].start()
        pending.extend(copies)
        return copies

    def end(index, step, copies):
        stages, spans, lands = states[index]
        back = step >= len(stages)
        at = 2 * len(stages) - 2 - step if back else step
        stage = stages[at]
        size, mine, _ = stage
        start, piece, slot = spans[at]
        if not back and at < len(stages) - 1:
            keep = rows_of(start + mine * piece, piece)
            total = acc[keep, :]
            for d, copy in enumerate(copies):
                copy.wait_recv()
                total = total + lands[at][d]
            acc[keep, :] = total
            return
        if not back:
            lands[at][mine] = acc[rows_of(start, piece), :]
        for d, (_, target) in enumerate(partners(stage)):
            sender = lax.rem(mine + size - 1 - d, size)
            if back:
                place = gat.at[rows_of(start + sender * piece, piece)]
                sems = send_g.at[index, slot + d], recv_g.at[index, slot + d]
            else:
                place = lands[at].at[sender]
                sems = send_s.at[index, slot + d], recv_s.at[index, slot + d]
            copy_to(place, place, *sems, target).wait_recv()
        if not back:
            total = lands[at][0]
            for q in range(1, size):
                total = total + lands[at][q]
            gat[rows_of(start, piece), :] = total

    steps = 2 * len(chunks[0]) - 1
    flying = [None, None]
    for step in range(steps):
        for index in range(2):
            if step > 0:
                end(index, step - 1, flying[index])
            flying[index] = begin(index, step)
        if step == (0 if kind == "all" else min(1, steps - 1)):
            start_rows()
            begin_cols()
        if step == max(steps - 2, 0):
            finish_rows()
    finish_cols()
    peak = jnp.max(jnp.sum(probe[0] * probe[0] + probe[1] * probe[1], axis=0))
    change = ext_out[...] / peak
    if kind == "all":
        rows_at = lax.broadcasted_iota(jnp.int32, (full_rows, full_cols), 0)
        cols_at = lax.broadcasted_iota(jnp.int32, (full_rows, full_cols), 1)
        first_row = jnp.where(me_row == 0, rim, 0)
        last_row = jnp.where(me_row == n_row - 1, full_rows - rim, full_rows)
        first_col = jnp.where(me_col == 0, rim, 0)
        last_col = jnp.where(me_col == n_col - 1, full_cols - rim, full_cols)
        inside = (rows_at >= first_row) & (rows_at < last_row)
        inside = inside & (cols_at >= first_col) & (cols_at < last_col)
        change = jnp.where(inside[None], change, 0.0)
    ext_out[...] = ext[...] + change
    for index in range(2):
        end(index, steps - 1, flying[index])

    weight = gat[pl.ds(2 * modes * pix, pix), :]
    for k in range(2):
        for m in range(modes):
            probe_out[k, m] = gat[pl.ds((k * modes + m) * pix, pix), :] / weight
    for copy in pending:
        copy.wait_send()
    drain()


def exchange(kind, ident, shape, pix, operands):
    rim = pix // 2
    full_rows, full_cols = shape[1], shape[2]
    wide = 2 * rim
    row_width = wide if kind == "all" else rim
    height = full_rows - wide if kind == "tile" else full_rows
    n_row, n_col = lax.axis_size("row"), lax.axis_size("col")
    side = (2, height, wide) if kind == "all" else (height, wide)
    scratch = [
        pltpu.VMEM(shape, jnp.float32),
        pltpu.VMEM((2, row_width, full_cols), jnp.float32),
        pltpu.VMEM((2, row_width, full_cols), jnp.float32),
    ]
    scratch += [pltpu.VMEM(side, jnp.float32)] * 4
    scratch += [pltpu.SemaphoreType.DMA((2, 3))] * 4
    out = jax.ShapeDtypeStruct(shape, jnp.float32)
    modes = 0
    if kind == "rim":
        outs = (out, jax.ShapeDtypeStruct((2, 2, 2 * pix, 2 * pix), jnp.bfloat16))
    else:
        probe, sums = operands[2:]
        modes = probe.shape[1]
        outs = (out, jax.ShapeDtypeStruct(probe.shape, jnp.float32))
        rows = sums.shape[0] * pix
        core, plane, far = col_factors(n_row, n_col)
        hops = core + plane + far - 3
        scratch += [pltpu.VMEM((rows, pix), jnp.float32)] * 2
        scratch += [pltpu.SemaphoreType.DMA((2, hops))] * 4
        for order in ((core, plane, far), (core, far, plane)):
            sizes = [f for f in order if f > 1]
            length = rows // 2
            for size in sizes[:-1]:
                length //= size
                scratch.append(pltpu.VMEM((size - 1, length, pix), jnp.float32))
            scratch.append(pltpu.VMEM((sizes[-1], length, pix), jnp.float32))
    return pl.pallas_call(
        functools.partial(exchange_kernel, kind, rim, modes, pix),
        out_shape=outs,
        in_specs=[VMEM] * len(operands),
        out_specs=tuple([VMEM] * len(outs)),
        scratch_shapes=scratch,
        compiler_params=pltpu.CompilerParams(
            collective_id=ident, has_side_effects=True, vmem_limit_bytes=LIMIT
        ),
        name="exchange_" + kind,
    )(*operands)


def on_device(object_field, probe, patterns, row_scales, positions, counts):
    modes, pix = probe.shape[1], probe.shape[2]
    rim = pix // 2
    starts = positions[0, 0].T
    amp = patterns[0, 0].astype(jnp.float32) * row_scales[0, 0][..., None]
    core, plane, far = col_factors(lax.axis_size("row"), lax.axis_size("col"))
    step = math.lcm(16 * core * max(plane, far), pix)
    rows_padded = -(-(2 * modes + 1) * pix // step) * step
    shape = (2, object_field.shape[1] + pix, object_field.shape[2] + pix)
    ext, table = exchange("rim", 0, shape, pix, (object_field,))
    for pass_number in range(PASSES):
        upd, sums = run_pass(ext, probe, amp, starts, counts, table, rows_padded)
        kind = "tile" if pass_number == PASSES - 1 else "all"
        ext, probe = exchange(kind, pass_number + 1, shape, pix, (upd, ext, probe, sums))
    return (ext[:, rim:-rim, rim:-rim], probe)


def solution(mesh):
    placed = (
        P(None, "row", "col"),
        P(),
        P("row", "col", None, None, None),
        P("row", "col", None, None),
        P("row", "col", None, None),
        P("row", "col"),
    )
    return jax.shard_map(
        on_device,
        mesh=mesh,
        in_specs=placed,
        out_specs=(P(None, "row", "col"), P()),
        check_vma=False,
    )
```
